32 devices in a mesh: groups: 2 (over y), rows: 4 (over z), chan: 2 (over x), sub: 2 (over core).
Axes of the slice: x: 2, y: 2, z: 4, core: 2. Of those that a mesh axis runs over, the one named last changes fastest.
Arguments:
- pair: bfloat16 [96, 48, 128], P(('groups', 'rows'), ('chan', 'sub')), parts along dimension 0, may hold values from -6 to 6
- res_mask: int32 [96], P('groups'), parts along dimension 0, may hold values 0 or 1
- out_ab: bfloat16 [128, 512], replicated, may hold values from -0.5 to 0.5
- out_gate: bfloat16 [128, 128], replicated, may hold values from -0.5 to 0.5
- out_proj: bfloat16 [128, 128], replicated, may hold values from -0.5 to 0.5
- in_ab: bfloat16 [128, 512], replicated, may hold values from -0.5 to 0.5
- in_gate: bfloat16 [128, 128], replicated, may hold values from -0.5 to 0.5
- in_proj: bfloat16 [128, 128], replicated, may hold values from -0.5 to 0.5
Outputs:
- updated: bfloat16 [96, 48, 128], P(('groups', 'rows'), ('chan', 'sub')), parts along dimension 0
The draws below stay inside these ranges and needn't reach their ends.
There are 2 independent parts, one for each index of `groups`. The reference program is written for one: setup_inputs(seed, part) draws one part's arguments, and reference() takes and returns one part's arrays. A program takes and returns all parts, laid end to end along the dimension named above; an argument that names none is the same for every part. Nothing has to cross between parts.
All inputs are finite; a program needn't handle non-finite values.
Results may differ from the reference program's by a relative error of at most 0.012.
Values may be sent and summed in bfloat16 or wider, within the bound.
A program may use at most 64 MiB of HBM per device.

```python
import jax
import jax.numpy as jnp
from jax import lax

C = 128
CH = 128
N = 48


def set_ends(array, stream_key, smallest, high):
    place = [jax.random.randint(jax.random.fold_in(stream_key, axis), (), 0, length) for axis, length in enumerate(array.shape)]
    longest = array.shape.index(max(array.shape))
    next_to = place[:longest] + [(place[longest] + 1) % array.shape[longest]] + place[longest + 1:]
    return array.at[tuple(place)].set(smallest).at[tuple(next_to)].set(high)


def steps_of(stream_key, dims, split, smallest, top_value):
    level, own = 1.0, jax.random.fold_in(stream_key, 6)
    for position, parts in split:
        steps = jnp.exp(jax.random.uniform(jax.random.fold_in(own, position), (parts,), jnp.float32, smallest / len(split), top_value / len(split)))
        level = level * jnp.repeat(steps, dims[position] // parts).reshape([-1 if axis == position else 1 for axis in range(len(dims))])
    return level


def scatter_about(key, extent, width, bound, cuts=(), held_as=jnp.bfloat16):
    array = width * jax.random.normal(key, extent, jnp.float32)
    if cuts:
        array = array * steps_of(key, extent, cuts, -0.22, 0.18)
    return jnp.clip(array, -bound, bound).astype(held_as)


def setup_inputs(seed: int = 0, part: int = 0) -> dict:
    streams_of = jax.random.split(jax.random.key(seed), 9)
    own_keys = jax.random.split(jax.random.fold_in(streams_of[8], part), 9)
    return {
        "pair": scatter_about(own_keys[0], (N, N, C), 1.0, 6.0, ((0, 4), (1, 4))),
        "res_mask": set_ends((jax.random.randint(own_keys[1], (N,), 0, 8) < 7).astype(jnp.int32), jax.random.fold_in(own_keys[1], 1), 0, 1),
        "out_ab": scatter_about(streams_of[2], (C, 4 * CH), C ** -0.5, 0.5),
        "out_gate": scatter_about(streams_of[3], (C, C), C ** -0.5, 0.5),
        "out_proj": scatter_about(streams_of[4], (CH, C), CH ** -0.5, 0.5),
        "in_ab": scatter_about(streams_of[5], (C, 4 * CH), C ** -0.5, 0.5),
        "in_gate": scatter_about(streams_of[6], (C, C), C ** -0.5, 0.5),
        "in_proj": scatter_about(streams_of[7], (CH, C), CH ** -0.5, 0.5),
    }


def normalize(values, axis):
    mean = lax.optimization_barrier(jnp.mean(values, axis=axis, keepdims=True))
    centered = values - mean
    var = lax.optimization_barrier(jnp.mean(centered * centered, axis=axis, keepdims=True))
    return centered * jax.lax.rsqrt(var + 1e-05)

def prepare(pair_in, res_mask, w_ab, w_gate):
    pair_f = pair_in.astype(jnp.float32)
    normed = normalize(pair_f, -1).astype(jnp.bfloat16).astype(jnp.float32)
    proj = jnp.einsum('ijc,cd->dij', normed, w_ab.astype(jnp.float32))
    maskf = res_mask.astype(jnp.float32)
    pair_mask = maskf[:, None] * maskf[None, :]
    left = (jax.nn.sigmoid(proj[:CH]) * proj[CH:2 * CH] * pair_mask).astype(jnp.bfloat16)
    right = (jax.nn.sigmoid(proj[2 * CH:3 * CH]) * proj[3 * CH:] * pair_mask).astype(jnp.bfloat16)
    gate = jax.nn.sigmoid(jnp.einsum('ijc,ce->ije', normed, w_gate.astype(jnp.float32)))
    return (pair_f, left, right, gate)

def finish(pair_f, tri, gate, w_proj):
    tnorm = normalize(tri.astype(jnp.float32), 0).astype(jnp.bfloat16).astype(jnp.float32)
    update = jnp.einsum('dij,de->ije', tnorm, w_proj.astype(jnp.float32))
    return (pair_f + gate * update).astype(jnp.bfloat16)

def reference(pair, res_mask, out_ab, out_gate, out_proj, in_ab, in_gate, in_proj):
    pair_f, left, right, gate = prepare(pair, res_mask, out_ab, out_gate)
    tri = jnp.einsum('dik,djk->dij', left.astype(jnp.float32), right.astype(jnp.float32)).astype(jnp.bfloat16)
    middle = finish(pair_f, tri, gate, out_proj)
    mid_f, left, right, gate = prepare(middle, res_mask, in_ab, in_gate)
    tri = jnp.einsum('dki,dkj->dij', left.astype(jnp.float32), right.astype(jnp.float32)).astype(jnp.bfloat16)
    return finish(mid_f, tri, gate, in_proj)
```

```python
import functools

import jax
import jax.numpy as jnp
from jax import lax
from jax.experimental import pallas as pl
from jax.experimental.pallas import tpu as pltpu
from jax.sharding import PartitionSpec as P


def normalize(values, axis):
    mean = jnp.mean(values, axis=axis, keepdims=True)
    centered = values - mean
    var = jnp.mean(centered * centered, axis=axis, keepdims=True)
    return centered * lax.rsqrt(var + 1e-05)


def prepare(pair_in, res_mask, w_ab, w_gate):
    row_count = pair_in.shape[0]
    col_count = pair_in.shape[1]
    hidden = w_ab.shape[1] // 4
    pair_f = pair_in.astype(jnp.float32)
    normed = normalize(pair_f, -1).astype(jnp.bfloat16)
    proj = jnp.einsum("ijc,cd->dij", normed, w_ab, preferred_element_type=jnp.float32)
    row_start = lax.axis_index("rows") * row_count
    col_start = lax.axis_index(("chan", "sub")) * col_count
    row_mask = lax.dynamic_slice_in_dim(res_mask, row_start, row_count).astype(jnp.float32)
    col_mask = lax.dynamic_slice_in_dim(res_mask, col_start, col_count).astype(jnp.float32)
    pair_mask = row_mask[:, None] * col_mask[None, :]
    left = (jax.nn.sigmoid(proj[:hidden]) * proj[hidden : 2 * hidden] * pair_mask).astype(
        jnp.bfloat16
    )
    right = (jax.nn.sigmoid(proj[2 * hidden : 3 * hidden]) * proj[3 * hidden :] * pair_mask).astype(
        jnp.bfloat16
    )
    gate = jax.nn.sigmoid(
        jnp.einsum("ijc,ce->ije", normed, w_gate, preferred_element_type=jnp.float32)
    )
    return (pair_f, left, right, gate)


def finish(pair_f, tri_local, gate, w_proj):
    tnorm = normalize(tri_local.astype(jnp.float32), 0).astype(jnp.bfloat16)
    update = jnp.einsum("dij,de->ije", tnorm, w_proj, preferred_element_type=jnp.float32)
    return (pair_f + gate * update).astype(jnp.bfloat16)


def on_device(pair, res_mask, out_ab, out_gate, out_proj, in_ab, in_gate, in_proj):
    pair_f, left, right, gate = prepare(pair, res_mask, out_ab, out_gate)
    left_grp, right_grp = (
        lax.all_to_all(left, ("chan", "sub"), split_axis=0, concat_axis=2, tiled=True),
        lax.all_to_all(right, ("chan", "sub"), split_axis=0, concat_axis=2, tiled=True),
    )
    tri = jnp.einsum(
        "dik,djk->dij",
        left_grp,
        lax.all_gather(right_grp, "rows", axis=1, tiled=True),
        preferred_element_type=jnp.float32,
    ).astype(jnp.bfloat16)
    tri_local = lax.all_to_all(tri, ("chan", "sub"), split_axis=2, concat_axis=0, tiled=True)
    middle = finish(pair_f, tri_local, gate, out_proj)
    mid_f, left, right, gate = prepare(middle, res_mask, in_ab, in_gate)
    left_grp, right_grp = (
        lax.all_to_all(left, ("chan", "sub"), split_axis=0, concat_axis=2, tiled=True),
        lax.all_to_all(right, ("chan", "sub"), split_axis=0, concat_axis=2, tiled=True),
    )
    left_turned = lax.all_to_all(left_grp, "rows", split_axis=2, concat_axis=1, tiled=True)
    tri = jnp.einsum(
        "dki,dkj->dij",
        left_turned,
        lax.all_gather(right_grp, "rows", axis=1, tiled=True),
        preferred_element_type=jnp.float32,
    ).astype(jnp.bfloat16)
    tri_local = lax.all_to_all(tri, ("chan", "sub"), split_axis=2, concat_axis=0, tiled=True)
    return finish(mid_f, tri_local, gate, in_proj)


MESH = pl.DeviceIdType.MESH


def sigmoid(x):
    return 0.5 * jnp.tanh(0.5 * x) + 0.5


def dot(x, y):
    return jnp.dot(x, y, preferred_element_type=jnp.float32)


def selection(shape, wide, narrow, turned):
    dense_axis = 0 if shape[0] == narrow * narrow else 1
    dense = lax.broadcasted_iota(jnp.int32, shape, dense_axis)
    padded = lax.broadcasted_iota(jnp.int32, shape, 1 - dense_axis)
    p, q = dense // narrow, dense % narrow
    place = q * wide + p if turned else p * wide + q
    return jnp.where(place == padded, 1.0, 0.0).astype(jnp.bfloat16)


def kernel(
    n,
    side,
    wide,
    pair_hbm,
    mask_ref,
    w_ab1_hbm,
    w_gate1_hbm,
    w_proj1_hbm,
    w_ab2_hbm,
    w_gate2_hbm,
    w_proj2_hbm,
    out_ref,
    pair_v,
    w_ab1,
    w_gate1,
    w_proj1,
    w_ab2,
    w_gate2,
    w_proj2,
    padded,
    left_wide,
    right_wide,
    a1,
    b1,
    b1_own,
    a2,
    a2_own,
    b2,
    in_sem,
    a1_send,
    a1_recv,
    b1_send,
    b1_recv,
    a2_send,
    a2_recv,
    b2_send,
    b2_recv,
):
    row = lax.axis_index("rows")
    subs = lax.axis_size("sub")
    col = lax.axis_index("chan") * subs + lax.axis_index("sub")

    def device(r, c):
        return {"rows": r, "chan": c // subs, "sub": c % subs}

    loads = []
    for place, (src, dst) in enumerate(
        (
            (pair_hbm, pair_v),
            (w_ab1_hbm, w_ab1),
            (w_gate1_hbm, w_gate1),
            (w_proj1_hbm, w_proj1),
            (w_ab2_hbm, w_ab2),
            (w_gate2_hbm, w_gate2),
            (w_proj2_hbm, w_proj2),
        )
    ):
        load = pltpu.make_async_copy(src, dst, in_sem.at[place])
        load.start()
        loads.append(load)

    barrier = pltpu.get_barrier_semaphore()
    for step in range(1, n * n):
        other = (row * n + col + step) % (n * n)
        pl.semaphore_signal(
            barrier, inc=1, device_id=device(other // n, other % n), device_id_type=MESH
        )

    squeeze = selection((side * side, side * wide), wide, side, False)
    squeeze_turned = selection((side * side, side * wide), wide, side, True)
    spread = selection((side * wide, side * side), wide, side, False)

    sublane = lax.broadcasted_iota(jnp.int32, (wide, pair_hbm.shape[-1]), 0)
    col_mask = jnp.zeros((wide, pair_hbm.shape[-1]), jnp.float32)
    for j in range(side):
        value = mask_ref[col * side + j].astype(jnp.float32)
        col_mask = jnp.where(sublane == j, value, col_mask)
    pair_mask = jnp.concatenate(
        [col_mask * mask_ref[row * side + i].astype(jnp.float32) for i in range(side)], axis=0
    )

    padded[...] = jnp.zeros_like(padded)
    loads[0].wait()
    padded[:, :side, :] = pair_v[...].astype(jnp.float32)
    pair_f = padded[...].reshape(side * wide, -1)

    def prepare(values, w_ab, w_gate, load_ab, load_gate):
        normed = normalize(values, -1).astype(jnp.bfloat16)
        load_ab.wait()
        proj = dot(normed, w_ab[...])
        hidden = w_ab.shape[1] // 4
        left = sigmoid(proj[:, :hidden]) * proj[:, hidden : 2 * hidden] * pair_mask
        right = sigmoid(proj[:, 2 * hidden : 3 * hidden]) * proj[:, 3 * hidden :] * pair_mask

        def gate():
            load_gate.wait()
            return sigmoid(dot(normed, w_gate[...]))

        return left.astype(jnp.bfloat16), right.astype(jnp.bfloat16), gate

    def finish(values, tri, gate, w_proj):
        tri = tri.astype(jnp.bfloat16).astype(jnp.float32)
        tnorm = normalize(tri, -1).astype(jnp.bfloat16)
        return (values + gate * dot(tnorm, w_proj[...])).astype(jnp.bfloat16)

    def send(src, buf, slot, send_sem, recv_sem, r, c):
        return pltpu.make_async_remote_copy(
            src_ref=src,
            dst_ref=buf.at[slot],
            send_sem=send_sem,
            recv_sem=recv_sem.at[slot],
            device_id=device(r, c),
            device_id_type=MESH,
        )

    def await_block(buf, slot, send_sem, recv_sem):
        send(buf.at[slot], buf, slot, send_sem, recv_sem, row, col).wait_recv()

    def add_products(total, left, right):
        left_wide[...] = dot(spread, left[...]).reshape(left_wide.shape)
        right_wide[...] = dot(spread, right[...]).reshape(right_wide.shape)

        def step(k, total):
            row_of_right = right_wide[k]
            return tuple(
                total[i] + left_wide[k, pl.ds(i, 1), :] * row_of_right for i in range(side)
            )

        return lax.fori_loop(0, side, step, total, unroll=True)

    def zeros():
        return tuple(
            jnp.zeros((wide, pair_hbm.shape[-1]), jnp.float32) for _ in range(side)
        )

    left, right, gate = prepare(pair_f, w_ab1, w_gate1, loads[1], loads[2])
    a1[col] = dot(squeeze_turned, left).astype(jnp.bfloat16)
    b1_own[...] = dot(squeeze_turned, right).astype(jnp.bfloat16)
    pl.semaphore_wait(barrier, n * n - 1)
    mine = row == col
    sends = []
    for s in range(1, n):
        copy = send(b1_own, b1, col, b1_send.at[s], b1_recv, (row + s) % n, row)
        copy.start()
        sends.append(copy)
    turn1 = send(b1_own, b1, col, b1_send.at[0], b1_recv, row, row)

    @pl.when(jnp.logical_not(mine))
    def _():
        turn1.start()

    for s in range(1, n):
        copy = send(a1.at[col], a1, col, a1_send.at[s], a1_recv, row, (col + s) % n)
        copy.start()
        sends.append(copy)

    @pl.when(mine)
    def _():
        b1[col] = b1_own[...]

    gate1 = gate()
    total = zeros()
    for s in range(n):
        block = (col + s) % n
        if s:
            await_block(a1, block, a1_send.at[0], a1_recv)
            await_block(b1, block, b1_send.at[0], b1_recv)
        else:

            @pl.when(jnp.logical_not(mine))
            def _():
                await_block(b1, block, b1_send.at[0], b1_recv)

        total = add_products(total, a1.at[block], b1.at[block])
    loads[3].wait()
    middle = finish(pair_f, jnp.concatenate(total, axis=0), gate1, w_proj1)

    mid_f = middle.astype(jnp.float32)
    left, right, gate = prepare(mid_f, w_ab2, w_gate2, loads[4], loads[5])
    b2[row] = dot(squeeze, right).astype(jnp.bfloat16)
    a2_own[...] = dot(squeeze, left).astype(jnp.bfloat16)
    for s in range(1, n):
        copy = send(b2.at[row], b2, row, b2_send.at[s], b2_recv, (row + s) % n, col)
        copy.start()
        sends.append(copy)
    for s in range(1, n):
        copy = send(a2_own, a2, row, a2_send.at[s], a2_recv, col, (col + s) % n)
        copy.start()
        sends.append(copy)
    turn2 = send(a2_own, a2, row, a2_send.at[0], a2_recv, col, col)

    @pl.when(jnp.logical_not(mine))
    def _():
        turn2.start()

    @pl.when(mine)
    def _():
        a2[row] = a2_own[...]

    gate2 = gate()
    total = zeros()
    for s in range(n):
        block = (row + s) % n
        if s:
            await_block(a2, block, a2_send.at[0], a2_recv)
            await_block(b2, block, b2_send.at[0], b2_recv)
        else:

            @pl.when(jnp.logical_not(mine))
            def _():
                await_block(a2, block, a2_send.at[0], a2_recv)

        total = add_products(total, a2.at[block], b2.at[block])
    loads[6].wait()
    updated = finish(mid_f, jnp.concatenate(total, axis=0), gate2, w_proj2)
    out_ref[...] = updated.reshape(side, wide, -1)[:, :side, :]
    for copy in sends:
        copy.wait_send()

    @pl.when(jnp.logical_not(mine))
    def _():
        turn1.wait_send()
        turn2.wait_send()


def on_square(n, pair, res_mask, *weights):
    side, _, channels = pair.shape
    wide = -(-side // 16) * 16
    block = (side * side, channels)
    blocks = pltpu.VMEM((n, *block), jnp.bfloat16)
    spread_out = pltpu.VMEM((side, wide, channels), jnp.float32)
    sems = pltpu.SemaphoreType.DMA((n,))
    anywhere = pl.BlockSpec(memory_space=pl.ANY)
    return pl.pallas_call(
        functools.partial(kernel, n, side, wide),
        out_shape=jax.ShapeDtypeStruct(pair.shape, pair.dtype),
        in_specs=[anywhere, pl.BlockSpec(memory_space=pltpu.SMEM)] + [anywhere] * len(weights),
        out_specs=pl.BlockSpec(memory_space=pltpu.VMEM),
        scratch_shapes=[pltpu.VMEM(pair.shape, pair.dtype)]
        + [pltpu.VMEM(w.shape, w.dtype) for w in weights]
        + [spread_out] * 3
        + [blocks, blocks, pltpu.VMEM(block, jnp.bfloat16)]
        + [blocks, pltpu.VMEM(block, jnp.bfloat16), blocks]
        + [pltpu.SemaphoreType.DMA((1 + len(weights),))]
        + [sems] * 8,
        compiler_params=pltpu.CompilerParams(
            collective_id=0, has_side_effects=True, vmem_limit_bytes=32 * 2**20
        ),
    )(pair, res_mask, *weights)


def solution(mesh):
    n = mesh.shape["rows"]
    square = n == mesh.shape["chan"] * mesh.shape["sub"]

    def per_device(pair, *rest):
        if square and pair.shape[0] == pair.shape[1] and pair.shape[0] <= 16:
            return on_square(n, pair, *rest)
        return on_device(pair, *rest)

    return jax.shard_map(
        per_device,
        mesh=mesh,
        in_specs=(
            P(("groups", "rows"), ("chan", "sub"), None),
            P("groups"),
            P(),
            P(),
            P(),
            P(),
            P(),
            P(),
        ),
        out_specs=P(("groups", "rows"), ("chan", "sub"), None),
        check_vma=False,
    )
```

```python
import functools

import jax
import jax.numpy as jnp
from jax import lax
from jax.experimental import pallas as pl
from jax.experimental.pallas import tpu as pltpu
from jax.sharding import PartitionSpec as P


def normalize(values, axis):
    mean = jnp.mean(values, axis=axis, keepdims=True)
    centered = values - mean
    var = jnp.mean(centered * centered, axis=axis, keepdims=True)
    return centered * lax.rsqrt(var + 1e-05)


def prepare(pair_in, res_mask, w_ab, w_gate):
    row_count = pair_in.shape[0]
    col_count = pair_in.shape[1]
    hidden = w_ab.shape[1] // 4
    pair_f = pair_in.astype(jnp.float32)
    normed = normalize(pair_f, -1).astype(jnp.bfloat16)
    proj = jnp.einsum("ijc,cd->dij", normed, w_ab, preferred_element_type=jnp.float32)
    row_start = lax.axis_index("rows") * row_count
    col_start = lax.axis_index(("chan", "sub")) * col_count
    row_mask = lax.dynamic_slice_in_dim(res_mask, row_start, row_count).astype(jnp.float32)
    col_mask = lax.dynamic_slice_in_dim(res_mask, col_start, col_count).astype(jnp.float32)
    pair_mask = row_mask[:, None] * col_mask[None, :]
    left = (jax.nn.sigmoid(proj[:hidden]) * proj[hidden : 2 * hidden] * pair_mask).astype(
        jnp.bfloat16
    )
    right = (jax.nn.sigmoid(proj[2 * hidden : 3 * hidden]) * proj[3 * hidden :] * pair_mask).astype(
        jnp.bfloat16
    )
    gate = jax.nn.sigmoid(
        jnp.einsum("ijc,ce->ije", normed, w_gate, preferred_element_type=jnp.float32)
    )
    return (pair_f, left, right, gate)


def finish(pair_f, tri_local, gate, w_proj):
    tnorm = normalize(tri_local.astype(jnp.float32), 0).astype(jnp.bfloat16)
    update = jnp.einsum("dij,de->ije", tnorm, w_proj, preferred_element_type=jnp.float32)
    return (pair_f + gate * update).astype(jnp.bfloat16)


def on_device(pair, res_mask, out_ab, out_gate, out_proj, in_ab, in_gate, in_proj):
    pair_f, left, right, gate = prepare(pair, res_mask, out_ab, out_gate)
    left_grp, right_grp = (
        lax.all_to_all(left, ("chan", "sub"), split_axis=0, concat_axis=2, tiled=True),
        lax.all_to_all(right, ("chan", "sub"), split_axis=0, concat_axis=2, tiled=True),
    )
    tri = jnp.einsum(
        "dik,djk->dij",
        left_grp,
        lax.all_gather(right_grp, "rows", axis=1, tiled=True),
        preferred_element_type=jnp.float32,
    ).astype(jnp.bfloat16)
    tri_local = lax.all_to_all(tri, ("chan", "sub"), split_axis=2, concat_axis=0, tiled=True)
    middle = finish(pair_f, tri_local, gate, out_proj)
    mid_f, left, right, gate = prepare(middle, res_mask, in_ab, in_gate)
    left_grp, right_grp = (
        lax.all_to_all(left, ("chan", "sub"), split_axis=0, concat_axis=2, tiled=True),
        lax.all_to_all(right, ("chan", "sub"), split_axis=0, concat_axis=2, tiled=True),
    )
    left_turned = lax.all_to_all(left_grp, "rows", split_axis=2, concat_axis=1, tiled=True)
    tri = jnp.einsum(
        "dki,dkj->dij",
        left_turned,
        lax.all_gather(right_grp, "rows", axis=1, tiled=True),
        preferred_element_type=jnp.float32,
    ).astype(jnp.bfloat16)
    tri_local = lax.all_to_all(tri, ("chan", "sub"), split_axis=2, concat_axis=0, tiled=True)
    return finish(mid_f, tri_local, gate, in_proj)


MESH = pl.DeviceIdType.MESH


def sigmoid(x):
    return 0.5 * jnp.tanh(0.5 * x) + 0.5


def dot(x, y):
    return jnp.dot(x, y, preferred_element_type=jnp.float32)


def selection(shape, wide, narrow, turned):
    dense_axis = 0 if shape[0] == narrow * narrow else 1
    dense = lax.broadcasted_iota(jnp.int32, shape, dense_axis)
    padded = lax.broadcasted_iota(jnp.int32, shape, 1 - dense_axis)
    p, q = dense // narrow, dense % narrow
    place = q * wide + p if turned else p * wide + q
    return jnp.where(place == padded, 1.0, 0.0).astype(jnp.bfloat16)


def kernel(
    n,
    side,
    wide,
    pair_hbm,
    mask_hbm,
    w_ab1_hbm,
    w_gate1_hbm,
    w_proj1_hbm,
    w_ab2_hbm,
    w_gate2_hbm,
    w_proj2_hbm,
    out_ref,
    pair_v,
    mask_ref,
    w_ab1,
    w_gate1,
    w_proj1,
    w_ab2,
    w_gate2,
    w_proj2,
    padded,
    left_wide,
    right_wide,
    a1,
    b1,
    b1_own,
    a2,
    a2_own,
    b2,
    in_sem,
    a1_send,
    a1_recv,
    b1_send,
    b1_recv,
    a2_send,
    a2_recv,
    b2_send,
    b2_recv,
):
    row = lax.axis_index("rows")
    subs = lax.axis_size("sub")
    col = lax.axis_index("chan") * subs + lax.axis_index("sub")

    def device(r, c):
        return {"rows": r, "chan": c // subs, "sub": c % subs}

    loads = []
    for place, (src, dst) in enumerate(
        (
            (pair_hbm, pair_v),
            (mask_hbm, mask_ref),
            (w_ab1_hbm, w_ab1),
            (w_gate1_hbm, w_gate1),
            (w_proj1_hbm, w_proj1),
            (w_ab2_hbm, w_ab2),
            (w_gate2_hbm, w_gate2),
            (w_proj2_hbm, w_proj2),
        )
    ):
        load = pltpu.make_async_copy(src, dst, in_sem.at[place])
        load.start()
        loads.append(load)

    barrier = pltpu.get_barrier_semaphore()
    for step in range(1, n * n):
        other = (row * n + col + step) % (n * n)
        pl.semaphore_signal(
            barrier, inc=1, device_id=device(other // n, other % n), device_id_type=MESH
        )

    squeeze = selection((side * side, side * wide), wide, side, False)
    squeeze_turned = selection((side * side, side * wide), wide, side, True)
    spread = selection((side * wide, side * side), wide, side, False)

    loads[1].wait()
    sublane = lax.broadcasted_iota(jnp.int32, (wide, pair_hbm.shape[-1]), 0)
    col_mask = jnp.zeros((wide, pair_hbm.shape[-1]), jnp.float32)
    for j in range(side):
        value = mask_ref[col * side + j].astype(jnp.float32)
        col_mask = jnp.where(sublane == j, value, col_mask)
    pair_mask = jnp.concatenate(
        [col_mask * mask_ref[row * side + i].astype(jnp.float32) for i in range(side)], axis=0
    )

    padded[...] = jnp.zeros_like(padded)
    loads[0].wait()
    padded[:, :side, :] = pair_v[...].astype(jnp.float32)
    pair_f = padded[...].reshape(side * wide, -1)

    def prepare(values, w_ab, w_gate, load_ab, load_gate):
        normed = normalize(values, -1).astype(jnp.bfloat16)
        load_ab.wait()
        proj = dot(normed, w_ab[...])
        hidden = w_ab.shape[1] // 4
        left = sigmoid(proj[:, :hidden]) * proj[:, hidden : 2 * hidden] * pair_mask
        right = sigmoid(proj[:, 2 * hidden : 3 * hidden]) * proj[:, 3 * hidden :] * pair_mask

        def gate():
            load_gate.wait()
            return sigmoid(dot(normed, w_gate[...]))

        return left.astype(jnp.bfloat16), right.astype(jnp.bfloat16), gate

    def finish(values, tri, gate, w_proj):
        tri = tri.astype(jnp.bfloat16).astype(jnp.float32)
        tnorm = normalize(tri, -1).astype(jnp.bfloat16)
        return (values + gate * dot(tnorm, w_proj[...])).astype(jnp.bfloat16)

    def send(src, buf, slot, send_sem, recv_sem, r, c):
        return pltpu.make_async_remote_copy(
            src_ref=src,
            dst_ref=buf.at[slot],
            send_sem=send_sem,
            recv_sem=recv_sem.at[slot],
            device_id=device(r, c),
            device_id_type=MESH,
        )

    def await_block(buf, slot, send_sem, recv_sem):
        send(buf.at[slot], buf, slot, send_sem, recv_sem, row, col).wait_recv()

    def add_products(total, left, right):
        left_wide[...] = dot(spread, left[...]).reshape(left_wide.shape)
        right_wide[...] = dot(spread, right[...]).reshape(right_wide.shape)

        def step(k, total):
            row_of_right = right_wide[k]
            return tuple(
                total[i] + left_wide[k, pl.ds(i, 1), :] * row_of_right for i in range(side)
            )

        return lax.fori_loop(0, side, step, total, unroll=True)

    def zeros():
        return tuple(
            jnp.zeros((wide, pair_hbm.shape[-1]), jnp.float32) for _ in range(side)
        )

    left, right, gate = prepare(pair_f, w_ab1, w_gate1, loads[2], loads[3])
    a1[col] = dot(squeeze_turned, left).astype(jnp.bfloat16)
    b1_own[...] = dot(squeeze_turned, right).astype(jnp.bfloat16)
    pl.semaphore_wait(barrier, n * n - 1)
    mine = row == col
    sends = []
    for s in range(1, n):
        copy = send(b1_own, b1, col, b1_send.at[s], b1_recv, (row + s) % n, row)
        copy.start()
        sends.append(copy)
    turn1 = send(b1_own, b1, col, b1_send.at[0], b1_recv, row, row)

    @pl.when(jnp.logical_not(mine))
    def _():
        turn1.start()

    for s in range(1, n):
        copy = send(a1.at[col], a1, col, a1_send.at[s], a1_recv, row, (col + s) % n)
        copy.start()
        sends.append(copy)

    @pl.when(mine)
    def _():
        b1[col] = b1_own[...]

    gate1 = gate()
    total = zeros()
    for s in range(n):
        block = (col + s) % n
        if s:
            await_block(a1, block, a1_send.at[0], a1_recv)
            await_block(b1, block, b1_send.at[0], b1_recv)
        else:

            @pl.when(jnp.logical_not(mine))
            def _():
                await_block(b1, block, b1_send.at[0], b1_recv)

        total = add_products(total, a1.at[block], b1.at[block])
    loads[4].wait()
    middle = finish(pair_f, jnp.concatenate(total, axis=0), gate1, w_proj1)

    mid_f = middle.astype(jnp.float32)
    left, right, gate = prepare(mid_f, w_ab2, w_gate2, loads[5], loads[6])
    b2[row] = dot(squeeze, right).astype(jnp.bfloat16)
    a2_own[...] = dot(squeeze, left).astype(jnp.bfloat16)
    for s in range(1, n):
        copy = send(b2.at[row], b2, row, b2_send.at[s], b2_recv, (row + s) % n, col)
        copy.start()
        sends.append(copy)
    for s in range(1, n):
        copy = send(a2_own, a2, row, a2_send.at[s], a2_recv, col, (col + s) % n)
        copy.start()
        sends.append(copy)
    turn2 = send(a2_own, a2, row, a2_send.at[0], a2_recv, col, col)

    @pl.when(jnp.logical_not(mine))
    def _():
        turn2.start()

    @pl.when(mine)
    def _():
        a2[row] = a2_own[...]

    gate2 = gate()
    total = zeros()
    for s in range(n):
        block = (row + s) % n
        if s:
            await_block(a2, block, a2_send.at[0], a2_recv)
            await_block(b2, block, b2_send.at[0], b2_recv)
        else:

            @pl.when(jnp.logical_not(mine))
            def _():
                await_block(a2, block, a2_send.at[0], a2_recv)

        total = add_products(total, a2.at[block], b2.at[block])
    loads[7].wait()
    updated = finish(mid_f, jnp.concatenate(total, axis=0), gate2, w_proj2)
    out_ref[...] = updated.reshape(side, wide, -1)[:, :side, :]
    for copy in sends:
        copy.wait_send()

    @pl.when(jnp.logical_not(mine))
    def _():
        turn1.wait_send()
        turn2.wait_send()


def on_square(n, pair, res_mask, *weights):
    side, _, channels = pair.shape
    wide = -(-side // 16) * 16
    block = (side * side, channels)
    blocks = pltpu.VMEM((n, *block), jnp.bfloat16)
    spread_out = pltpu.VMEM((side, wide, channels), jnp.float32)
    sems = pltpu.SemaphoreType.DMA((n,))
    in_hbm = pl.BlockSpec(memory_space=pltpu.HBM)
    return pl.pallas_call(
        functools.partial(kernel, n, side, wide),
        out_shape=jax.ShapeDtypeStruct(pair.shape, pair.dtype),
        in_specs=[in_hbm] * (2 + len(weights)),
        out_specs=pl.BlockSpec(memory_space=pltpu.VMEM),
        scratch_shapes=[pltpu.VMEM(pair.shape, pair.dtype)]
        + [pltpu.SMEM(res_mask.shape, res_mask.dtype)]
        + [pltpu.VMEM(w.shape, w.dtype) for w in weights]
        + [spread_out] * 3
        + [blocks, blocks, pltpu.VMEM(block, jnp.bfloat16)]
        + [blocks, pltpu.VMEM(block, jnp.bfloat16), blocks]
        + [pltpu.SemaphoreType.DMA((2 + len(weights),))]
        + [sems] * 8,
        compiler_params=pltpu.CompilerParams(
            collective_id=0, has_side_effects=True, vmem_limit_bytes=60 * 2**20
        ),
    )(pair, res_mask, *weights)


def solution(mesh):
    n = mesh.shape["rows"]
    square = n == mesh.shape["chan"] * mesh.shape["sub"]

    def per_device(pair, *rest):
        if square and pair.shape[0] == pair.shape[1] and pair.shape[0] <= 16:
            return on_square(n, pair, *rest)
        return on_device(pair, *rest)

    return jax.shard_map(
        per_device,
        mesh=mesh,
        in_specs=(
            P(("groups", "rows"), ("chan", "sub"), None),
            P("groups"),
            P(),
            P(),
            P(),
            P(),
            P(),
            P(),
        ),
        out_specs=P(("groups", "rows"), ("chan", "sub"), None),
        check_vma=False,
    )
```

```python
import functools

import jax
import jax.numpy as jnp
from jax import lax
from jax.experimental import pallas as pl
from jax.experimental.pallas import tpu as pltpu
from jax.sharding import PartitionSpec as P


def normalize(values, axis):
    mean = jnp.mean(values, axis=axis, keepdims=True)
    centered = values - mean
    var = jnp.mean(centered * centered, axis=axis, keepdims=True)
    return centered * lax.rsqrt(var + 1e-05)


def prepare(pair_in, res_mask, w_ab, w_gate):
    row_count = pair_in.shape[0]
    col_count = pair_in.shape[1]
    hidden = w_ab.shape[1] // 4
    pair_f = pair_in.astype(jnp.float32)
    normed = normalize(pair_f, -1).astype(jnp.bfloat16)
    proj = jnp.einsum("ijc,cd->dij", normed, w_ab, preferred_element_type=jnp.float32)
    row_start = lax.axis_index("rows") * row_count
    col_start = lax.axis_index(("chan", "sub")) * col_count
    row_mask = lax.dynamic_slice_in_dim(res_mask, row_start, row_count).astype(jnp.float32)
    col_mask = lax.dynamic_slice_in_dim(res_mask, col_start, col_count).astype(jnp.float32)
    pair_mask = row_mask[:, None] * col_mask[None, :]
    left = (jax.nn.sigmoid(proj[:hidden]) * proj[hidden : 2 * hidden] * pair_mask).astype(
        jnp.bfloat16
    )
    right = (jax.nn.sigmoid(proj[2 * hidden : 3 * hidden]) * proj[3 * hidden :] * pair_mask).astype(
        jnp.bfloat16
    )
    gate = jax.nn.sigmoid(
        jnp.einsum("ijc,ce->ije", normed, w_gate, preferred_element_type=jnp.float32)
    )
    return (pair_f, left, right, gate)


def finish(pair_f, tri_local, gate, w_proj):
    tnorm = normalize(tri_local.astype(jnp.float32), 0).astype(jnp.bfloat16)
    update = jnp.einsum("dij,de->ije", tnorm, w_proj, preferred_element_type=jnp.float32)
    return (pair_f + gate * update).astype(jnp.bfloat16)


def on_device(pair, res_mask, out_ab, out_gate, out_proj, in_ab, in_gate, in_proj):
    pair_f, left, right, gate = prepare(pair, res_mask, out_ab, out_gate)
    left_grp, right_grp = (
        lax.all_to_all(left, ("chan", "sub"), split_axis=0, concat_axis=2, tiled=True),
        lax.all_to_all(right, ("chan", "sub"), split_axis=0, concat_axis=2, tiled=True),
    )
    tri = jnp.einsum(
        "dik,djk->dij",
        left_grp,
        lax.all_gather(right_grp, "rows", axis=1, tiled=True),
        preferred_element_type=jnp.float32,
    ).astype(jnp.bfloat16)
    tri_local = lax.all_to_all(tri, ("chan", "sub"), split_axis=2, concat_axis=0, tiled=True)
    middle = finish(pair_f, tri_local, gate, out_proj)
    mid_f, left, right, gate = prepare(middle, res_mask, in_ab, in_gate)
    left_grp, right_grp = (
        lax.all_to_all(left, ("chan", "sub"), split_axis=0, concat_axis=2, tiled=True),
        lax.all_to_all(right, ("chan", "sub"), split_axis=0, concat_axis=2, tiled=True),
    )
    left_turned = lax.all_to_all(left_grp, "rows", split_axis=2, concat_axis=1, tiled=True)
    tri = jnp.einsum(
        "dki,dkj->dij",
        left_turned,
        lax.all_gather(right_grp, "rows", axis=1, tiled=True),
        preferred_element_type=jnp.float32,
    ).astype(jnp.bfloat16)
    tri_local = lax.all_to_all(tri, ("chan", "sub"), split_axis=2, concat_axis=0, tiled=True)
    return finish(mid_f, tri_local, gate, in_proj)


MESH = pl.DeviceIdType.MESH


def sigmoid(x):
    return 0.5 * jnp.tanh(0.5 * x) + 0.5


def dot(x, y):
    return jnp.dot(x, y, preferred_element_type=jnp.float32)


def selection(shape, wide, narrow, turned):
    dense_axis = 0 if shape[0] == narrow * narrow else 1
    dense = lax.broadcasted_iota(jnp.int32, shape, dense_axis)
    padded = lax.broadcasted_iota(jnp.int32, shape, 1 - dense_axis)
    p, q = dense // narrow, dense % narrow
    place = q * wide + p if turned else p * wide + q
    return jnp.where(place == padded, 1.0, 0.0).astype(jnp.bfloat16)


def kernel(
    n,
    side,
    wide,
    pair_hbm,
    mask_hbm,
    w_ab1_hbm,
    w_gate1_hbm,
    w_proj1_hbm,
    w_ab2_hbm,
    w_gate2_hbm,
    w_proj2_hbm,
    out_ref,
    pair_v,
    mask_ref,
    w_ab1,
    w_gate1,
    w_proj1,
    w_ab2,
    w_gate2,
    w_proj2,
    padded,
    left_wide,
    right_wide,
    pair_t,
    a1,
    a1_own,
    b1,
    mid_t,
    mid_own,
    a2,
    b2,
    b2_own,
    in_sem,
    t_send,
    t_recv,
    a1_send,
    a1_recv,
    b1_send,
    b1_recv,
    a2_send,
    a2_recv,
    b2_send,
    b2_recv,
):
    row = lax.axis_index("rows")
    subs = lax.axis_size("sub")
    col = lax.axis_index("chan") * subs + lax.axis_index("sub")
    mine = row == col
    channels = pair_hbm.shape[-1]

    def device(r, c):
        return {"rows": r, "chan": c // subs, "sub": c % subs}

    loads = []
    for place, (src, dst) in enumerate(
        (
            (pair_hbm, pair_v),
            (mask_hbm, mask_ref),
            (w_ab1_hbm, w_ab1),
            (w_gate1_hbm, w_gate1),
            (w_proj1_hbm, w_proj1),
            (w_ab2_hbm, w_ab2),
            (w_gate2_hbm, w_gate2),
            (w_proj2_hbm, w_proj2),
        )
    ):
        load = pltpu.make_async_copy(src, dst, in_sem.at[place])
        load.start()
        loads.append(load)

    barrier = pltpu.get_barrier_semaphore()
    for step in range(1, n * n):
        other = (row * n + col + step) % (n * n)
        pl.semaphore_signal(
            barrier, inc=1, device_id=device(other // n, other % n), device_id_type=MESH
        )

    squeeze = selection((side * side, side * wide), wide, side, False)
    squeeze_turned = selection((side * side, side * wide), wide, side, True)
    spread = selection((side * wide, side * side), wide, side, False)

    def tile_mask(rows, cols):
        sublane = lax.broadcasted_iota(jnp.int32, (wide, channels), 0)
        col_mask = jnp.zeros((wide, channels), jnp.float32)
        for j in range(side):
            value = mask_ref[cols * side + j].astype(jnp.float32)
            col_mask = jnp.where(sublane == j, value, col_mask)
        return jnp.concatenate(
            [col_mask * mask_ref[rows * side + i].astype(jnp.float32) for i in range(side)],
            axis=0,
        )

    def widen(block):
        padded[:, :side, :] = block[...].astype(jnp.float32)
        return padded[...].reshape(side * wide, channels)

    def norm(values):
        return normalize(values, -1).astype(jnp.bfloat16)

    def gated(normed, w_ab, half, mask):
        hidden = w_ab.shape[1] // 4
        proj = dot(normed, w_ab[:, 2 * half * hidden : 2 * (half + 1) * hidden])
        return (sigmoid(proj[:, :hidden]) * proj[:, hidden:] * mask).astype(jnp.bfloat16)

    def finish(values, total, gate, w_proj):
        tri = jnp.concatenate(total, axis=0).astype(jnp.bfloat16).astype(jnp.float32)
        return (values + gate * dot(norm(tri), w_proj[...])).astype(jnp.bfloat16)

    def send(src, dst, send_sem, recv_sem, r, c):
        return pltpu.make_async_remote_copy(
            src_ref=src,
            dst_ref=dst,
            send_sem=send_sem,
            recv_sem=recv_sem,
            device_id=device(r, c),
            device_id_type=MESH,
        )

    sends = []

    def spread_out(along, along_buf, along_sems, turn, turn_buf, turn_sems):
        for s in range(1, n):
            copy = send(
                turn, turn_buf.at[col], turn_sems[0].at[s], turn_sems[1].at[col], (col + s) % n, row
            )
            copy.start()
            sends.append(copy)
        for s in range(1, n):
            copy = send(
                along, along_buf.at[col], along_sems[0].at[s], along_sems[1].at[col], row, (col + s) % n
            )
            copy.start()
            sends.append(copy)

    def await_block(buf, slot, sems):
        send(buf.at[slot], buf.at[slot], sems[0].at[0], sems[1].at[slot], row, col).wait_recv()

    def widen_block(dst, block):
        dst[...] = dot(spread, block[...]).reshape(dst.shape)

    def add_products(total):
        def step(k, total):
            row_of_right = right_wide[k]
            return tuple(
                total[i] + left_wide[k, pl.ds(i, 1), :] * row_of_right for i in range(side)
            )

        return lax.fori_loop(0, side, step, total, unroll=True)

    def zeros():
        return tuple(jnp.zeros((wide, channels), jnp.float32) for _ in range(side))

    def contract(along, along_wide, along_sems, turn, turn_wide, turn_sems):
        total = zeros()
        for s in range(n):
            block = (row + s) % n
            if s:
                await_block(turn, block, turn_sems)
                widen_block(turn_wide, turn.at[block])

            @pl.when(block != col)
            def _():
                await_block(along, block, along_sems)

            widen_block(along_wide, along.at[block])
            total = add_products(total)
        return total

    a1_sems, b1_sems = (a1_send, a1_recv), (b1_send, b1_recv)
    a2_sems, b2_sems = (a2_send, a2_recv), (b2_send, b2_recv)
    padded[...] = jnp.zeros_like(padded)
    loads[0].wait()
    pair_f = widen(pair_v)
    normed = norm(pair_f)
    loads[1].wait()
    mask = tile_mask(row, col)
    mask_t = tile_mask(col, row)
    loads[2].wait()
    left = gated(normed, w_ab1, 0, mask)
    right = gated(normed, w_ab1, 1, mask)
    a1_own[...] = dot(squeeze_turned, left).astype(jnp.bfloat16)
    b1[col] = dot(squeeze_turned, right).astype(jnp.bfloat16)

    pl.semaphore_wait(barrier, n * n - 1)
    turn_pair = send(pair_hbm, pair_t, t_send.at[0], t_recv.at[0], col, row)
    stay_pair = pltpu.make_async_copy(pair_hbm, pair_t, t_send.at[0])

    @pl.when(jnp.logical_not(mine))
    def _():
        turn_pair.start()

    @pl.when(mine)
    def _():
        stay_pair.start()

    spread_out(b1.at[col], b1, b1_sems, a1_own, a1, a1_sems)

    @pl.when(jnp.logical_not(mine))
    def _():
        turn_pair.wait_recv()

    @pl.when(mine)
    def _():
        stay_pair.wait()

    pair_f = widen(pair_t)
    normed = norm(pair_f)
    turned = dot(squeeze_turned, gated(normed, w_ab1, 0, mask_t)).astype(jnp.bfloat16)
    left_wide[...] = dot(spread, turned).reshape(left_wide.shape)
    loads[3].wait()
    gate = sigmoid(dot(normed, w_gate1[...]))
    total = contract(b1, right_wide, b1_sems, a1, left_wide, a1_sems)
    loads[4].wait()
    middle = finish(pair_f, total, gate, w_proj1)

    mid_own[...] = dot(squeeze, middle).astype(jnp.bfloat16)
    turn_mid = send(mid_own, mid_t, t_send.at[1], t_recv.at[1], col, row)

    @pl.when(jnp.logical_not(mine))
    def _():
        turn_mid.start()

    normed = norm(middle.astype(jnp.float32))
    loads[5].wait()
    b2_own[...] = dot(squeeze, gated(normed, w_ab2, 1, mask_t)).astype(jnp.bfloat16)
    a2[col] = dot(squeeze, gated(normed, w_ab2, 0, mask_t)).astype(jnp.bfloat16)
    spread_out(a2.at[col], a2, a2_sems, b2_own, b2, b2_sems)

    @pl.when(jnp.logical_not(mine))
    def _():
        turn_mid.wait_recv()

    @pl.when(mine)
    def _():
        mid_t[...] = mid_own[...]

    mid_f = dot(spread, mid_t[...])
    normed = norm(mid_f)
    right_wide[...] = gated(normed, w_ab2, 1, mask).astype(jnp.float32).reshape(right_wide.shape)
    loads[6].wait()
    gate = sigmoid(dot(normed, w_gate2[...]))
    total = contract(a2, left_wide, a2_sems, b2, right_wide, b2_sems)
    loads[7].wait()
    updated = finish(mid_f, total, gate, w_proj2)
    out_ref[...] = updated.reshape(side, wide, channels)[:, :side, :]
    for copy in sends:
        copy.wait_send()

    @pl.when(jnp.logical_not(mine))
    def _():
        turn_pair.wait_send()
        turn_mid.wait_send()


def on_square(n, pair, res_mask, *weights):
    side, _, channels = pair.shape
    wide = -(-side // 16) * 16
    block = pltpu.VMEM((side * side, channels), jnp.bfloat16)
    blocks = pltpu.VMEM((n, side * side, channels), jnp.bfloat16)
    positions = pltpu.VMEM((side, wide, channels), jnp.float32)
    tile = pltpu.VMEM(pair.shape, pair.dtype)
    sems = pltpu.SemaphoreType.DMA((n,))
    in_hbm = pl.BlockSpec(memory_space=pltpu.HBM)
    return pl.pallas_call(
        functools.partial(kernel, n, side, wide),
        out_shape=jax.ShapeDtypeStruct(pair.shape, pair.dtype),
        in_specs=[in_hbm] * (2 + len(weights)),
        out_specs=pl.BlockSpec(memory_space=pltpu.VMEM),
        scratch_shapes=[tile, pltpu.SMEM(res_mask.shape, res_mask.dtype)]
        + [pltpu.VMEM(w.shape, w.dtype) for w in weights]
        + [positions] * 3
        + [tile, blocks, block, blocks]
        + [block, block, blocks, blocks, block]
        + [pltpu.SemaphoreType.DMA((2 + len(weights),))]
        + [pltpu.SemaphoreType.DMA((2,))] * 2
        + [sems] * 8,
        compiler_params=pltpu.CompilerParams(
            collective_id=0, has_side_effects=True, vmem_limit_bytes=60 * 2**20
        ),
    )(pair, res_mask, *weights)


def solution(mesh):
    n = mesh.shape["rows"]
    square = n == mesh.shape["chan"] * mesh.shape["sub"]

    def per_device(pair, *rest):
        if square and pair.shape[0] == pair.shape[1] and pair.shape[0] <= 16:
            return on_square(n, pair, *rest)
        return on_device(pair, *rest)

    return jax.shard_map(
        per_device,
        mesh=mesh,
        in_specs=(
            P(("groups", "rows"), ("chan", "sub"), None),
            P("groups"),
            P(),
            P(),
            P(),
            P(),
            P(),
            P(),
        ),
        out_specs=P(("groups", "rows"), ("chan", "sub"), None),
        check_vma=False,
    )
```

```python
import functools

import jax
import jax.numpy as jnp
from jax import lax
from jax.experimental import pallas as pl
from jax.experimental.pallas import tpu as pltpu
from jax.sharding import PartitionSpec as P


def normalize(values, axis):
    mean = jnp.mean(values, axis=axis, keepdims=True)
    centered = values - mean
    var = jnp.mean(centered * centered, axis=axis, keepdims=True)
    return centered * lax.rsqrt(var + 1e-05)


def prepare(pair_in, res_mask, w_ab, w_gate):
    row_count = pair_in.shape[0]
    col_count = pair_in.shape[1]
    hidden = w_ab.shape[1] // 4
    pair_f = pair_in.astype(jnp.float32)
    normed = normalize(pair_f, -1).astype(jnp.bfloat16)
    proj = jnp.einsum("ijc,cd->dij", normed, w_ab, preferred_element_type=jnp.float32)
    row_start = lax.axis_index("rows") * row_count
    col_start = lax.axis_index(("chan", "sub")) * col_count
    row_mask = lax.dynamic_slice_in_dim(res_mask, row_start, row_count).astype(jnp.float32)
    col_mask = lax.dynamic_slice_in_dim(res_mask, col_start, col_count).astype(jnp.float32)
    pair_mask = row_mask[:, None] * col_mask[None, :]
    left = (jax.nn.sigmoid(proj[:hidden]) * proj[hidden : 2 * hidden] * pair_mask).astype(
        jnp.bfloat16
    )
    right = (jax.nn.sigmoid(proj[2 * hidden : 3 * hidden]) * proj[3 * hidden :] * pair_mask).astype(
        jnp.bfloat16
    )
    gate = jax.nn.sigmoid(
        jnp.einsum("ijc,ce->ije", normed, w_gate, preferred_element_type=jnp.float32)
    )
    return (pair_f, left, right, gate)


def finish(pair_f, tri_local, gate, w_proj):
    tnorm = normalize(tri_local.astype(jnp.float32), 0).astype(jnp.bfloat16)
    update = jnp.einsum("dij,de->ije", tnorm, w_proj, preferred_element_type=jnp.float32)
    return (pair_f + gate * update).astype(jnp.bfloat16)


def on_device(pair, res_mask, out_ab, out_gate, out_proj, in_ab, in_gate, in_proj):
    pair_f, left, right, gate = prepare(pair, res_mask, out_ab, out_gate)
    left_grp, right_grp = (
        lax.all_to_all(left, ("chan", "sub"), split_axis=0, concat_axis=2, tiled=True),
        lax.all_to_all(right, ("chan", "sub"), split_axis=0, concat_axis=2, tiled=True),
    )
    tri = jnp.einsum(
        "dik,djk->dij",
        left_grp,
        lax.all_gather(right_grp, "rows", axis=1, tiled=True),
        preferred_element_type=jnp.float32,
    ).astype(jnp.bfloat16)
    tri_local = lax.all_to_all(tri, ("chan", "sub"), split_axis=2, concat_axis=0, tiled=True)
    middle = finish(pair_f, tri_local, gate, out_proj)
    mid_f, left, right, gate = prepare(middle, res_mask, in_ab, in_gate)
    left_grp, right_grp = (
        lax.all_to_all(left, ("chan", "sub"), split_axis=0, concat_axis=2, tiled=True),
        lax.all_to_all(right, ("chan", "sub"), split_axis=0, concat_axis=2, tiled=True),
    )
    left_turned = lax.all_to_all(left_grp, "rows", split_axis=2, concat_axis=1, tiled=True)
    tri = jnp.einsum(
        "dki,dkj->dij",
        left_turned,
        lax.all_gather(right_grp, "rows", axis=1, tiled=True),
        preferred_element_type=jnp.float32,
    ).astype(jnp.bfloat16)
    tri_local = lax.all_to_all(tri, ("chan", "sub"), split_axis=2, concat_axis=0, tiled=True)
    return finish(mid_f, tri_local, gate, in_proj)


MESH = pl.DeviceIdType.MESH


def sigmoid(x):
    return 0.5 * jnp.tanh(0.5 * x) + 0.5


def dot(x, y):
    return jnp.dot(x, y, preferred_element_type=jnp.float32)


def selection(shape, wide, narrow, turned):
    dense_axis = 0 if shape[0] == narrow * narrow else 1
    dense = lax.broadcasted_iota(jnp.int32, shape, dense_axis)
    padded = lax.broadcasted_iota(jnp.int32, shape, 1 - dense_axis)
    p, q = dense // narrow, dense % narrow
    place = q * wide + p if turned else p * wide + q
    return jnp.where(place == padded, 1.0, 0.0).astype(jnp.bfloat16)


def kernel(
    n,
    side,
    wide,
    pair_hbm,
    mask_hbm,
    w_ab1_hbm,
    w_gate1_hbm,
    w_proj1_hbm,
    w_ab2_hbm,
    w_gate2_hbm,
    w_proj2_hbm,
    out_ref,
    pair_v,
    mask_ref,
    w_ab1,
    w_gate1,
    w_proj1,
    w_ab2,
    w_gate2,
    w_proj2,
    padded,
    left_wide,
    right_wide,
    mask,
    mask_t,
    squeeze,
    squeeze_turned,
    spread,
    pair_t,
    a1,
    a1_own,
    b1,
    mid_t,
    mid_own,
    a2,
    b2,
    b2_own,
    in_sem,
    t_send,
    t_recv,
    a1_send,
    a1_recv,
    b1_send,
    b1_recv,
    a2_send,
    a2_recv,
    b2_send,
    b2_recv,
):
    row = lax.axis_index("rows")
    subs = lax.axis_size("sub")
    col = lax.axis_index("chan") * subs + lax.axis_index("sub")
    mine = row == col
    channels = pair_hbm.shape[-1]

    def device(r, c):
        return {"rows": r, "chan": c // subs, "sub": c % subs}

    loads = []
    for place, (src, dst) in enumerate(
        (
            (pair_hbm, pair_v),
            (mask_hbm, mask_ref),
            (w_ab1_hbm, w_ab1),
            (w_gate1_hbm, w_gate1),
            (w_proj1_hbm, w_proj1),
            (w_ab2_hbm, w_ab2),
            (w_gate2_hbm, w_gate2),
            (w_proj2_hbm, w_proj2),
        )
    ):
        load = pltpu.make_async_copy(src, dst, in_sem.at[place])
        load.start()
        loads.append(load)

    barrier = pltpu.get_barrier_semaphore()
    for step in range(1, n):
        pl.semaphore_signal(
            barrier, inc=1, device_id=device(col, (row + step) % n), device_id_type=MESH
        )
    for step in range(1, n):
        pl.semaphore_signal(
            barrier, inc=1, device_id=device(row, (col + step) % n), device_id_type=MESH
        )

    @pl.when(jnp.logical_not(mine))
    def _():
        pl.semaphore_signal(barrier, inc=1, device_id=device(col, row), device_id_type=MESH)

    squeeze[...] = selection((side * side, side * wide), wide, side, False)
    squeeze_turned[...] = selection((side * side, side * wide), wide, side, True)
    spread[...] = selection((side * wide, side * side), wide, side, False)

    def tile_mask(rows, cols):
        sublane = lax.broadcasted_iota(jnp.int32, (wide, channels), 0)
        col_mask = jnp.zeros((wide, channels), jnp.float32)
        for j in range(side):
            value = mask_ref[cols * side + j].astype(jnp.float32)
            col_mask = jnp.where(sublane == j, value, col_mask)
        return jnp.concatenate(
            [col_mask * mask_ref[rows * side + i].astype(jnp.float32) for i in range(side)],
            axis=0,
        )

    def widen(block):
        padded[:, :side, :] = block[...].astype(jnp.float32)
        return padded[...].reshape(side * wide, channels)

    def norm(values):
        return normalize(values, -1).astype(jnp.bfloat16)

    def gated(normed, w_ab, half, mask):
        hidden = w_ab.shape[1] // 4
        proj = dot(normed, w_ab[:, 2 * half * hidden : 2 * (half + 1) * hidden])
        return (sigmoid(proj[:, :hidden]) * proj[:, hidden:] * mask[...]).astype(jnp.bfloat16)

    def finish(values, total, gate, w_proj):
        tri = jnp.concatenate(total, axis=0).astype(jnp.bfloat16).astype(jnp.float32)
        return (values + gate * dot(norm(tri), w_proj[...])).astype(jnp.bfloat16)

    def send(src, dst, send_sem, recv_sem, r, c):
        return pltpu.make_async_remote_copy(
            src_ref=src,
            dst_ref=dst,
            send_sem=send_sem,
            recv_sem=recv_sem,
            device_id=device(r, c),
            device_id_type=MESH,
        )

    sends = []

    def spread_out(along, along_buf, along_sems, turn, turn_buf, turn_sems):
        for s in range(1, n):
            copy = send(
                turn, turn_buf.at[col], turn_sems[0].at[s], turn_sems[1].at[col], (col + s) % n, row
            )
            copy.start()
            sends.append(copy)
        for s in range(1, n):
            copy = send(
                along, along_buf.at[col], along_sems[0].at[s], along_sems[1].at[col], row, (col + s) % n
            )
            copy.start()
            sends.append(copy)

    def await_block(buf, slot, sems):
        send(buf.at[slot], buf.at[slot], sems[0].at[0], sems[1].at[slot], row, col).wait_recv()

    def widen_block(dst, block):
        dst[...] = dot(spread[...], block[...]).reshape(dst.shape)

    def add_products(total):
        def step(k, total):
            row_of_right = right_wide[k]
            return tuple(
                total[i] + left_wide[k, pl.ds(i, 1), :] * row_of_right for i in range(side)
            )

        return lax.fori_loop(0, side, step, total, unroll=True)

    def zeros():
        return tuple(jnp.zeros((wide, channels), jnp.float32) for _ in range(side))

    def contract(along, along_wide, along_sems, turn, turn_wide, turn_sems):
        total = zeros()
        for s in range(n):
            block = (row + s) % n
            if s:
                await_block(turn, block, turn_sems)
                widen_block(turn_wide, turn.at[block])

            @pl.when(block != col)
            def _():
                await_block(along, block, along_sems)

            widen_block(along_wide, along.at[block])
            total = add_products(total)
        return total

    a1_sems, b1_sems = (a1_send, a1_recv), (b1_send, b1_recv)
    a2_sems, b2_sems = (a2_send, a2_recv), (b2_send, b2_recv)
    padded[...] = jnp.zeros_like(padded)
    loads[0].wait()
    pair_f = widen(pair_v)
    normed = norm(pair_f)
    loads[1].wait()
    mask[...] = tile_mask(row, col)
    mask_t[...] = tile_mask(col, row)
    loads[2].wait()
    left = gated(normed, w_ab1, 0, mask)
    right = gated(normed, w_ab1, 1, mask)
    a1_own[...] = dot(squeeze_turned[...], left).astype(jnp.bfloat16)
    b1[col] = dot(squeeze_turned[...], right).astype(jnp.bfloat16)

    @pl.when(mine)
    def _():
        pl.semaphore_wait(barrier, 2 * (n - 1))

    @pl.when(jnp.logical_not(mine))
    def _():
        pl.semaphore_wait(barrier, 2 * n - 1)

    turn_pair = send(pair_hbm, pair_t, t_send.at[0], t_recv.at[0], col, row)
    stay_pair = pltpu.make_async_copy(pair_hbm, pair_t, t_send.at[0])

    @pl.when(jnp.logical_not(mine))
    def _():
        turn_pair.start()

    @pl.when(mine)
    def _():
        stay_pair.start()

    spread_out(b1.at[col], b1, b1_sems, a1_own, a1, a1_sems)

    @pl.when(jnp.logical_not(mine))
    def _():
        turn_pair.wait_recv()

    @pl.when(mine)
    def _():
        stay_pair.wait()

    pair_f = widen(pair_t)
    normed = norm(pair_f)
    turned = dot(squeeze_turned[...], gated(normed, w_ab1, 0, mask_t)).astype(jnp.bfloat16)
    left_wide[...] = dot(spread[...], turned).reshape(left_wide.shape)
    loads[3].wait()
    gate = sigmoid(dot(normed, w_gate1[...]))
    total = contract(b1, right_wide, b1_sems, a1, left_wide, a1_sems)
    loads[4].wait()
    middle = finish(pair_f, total, gate, w_proj1)

    mid_own[...] = dot(squeeze[...], middle).astype(jnp.bfloat16)
    turn_mid = send(mid_own, mid_t, t_send.at[1], t_recv.at[1], col, row)

    @pl.when(jnp.logical_not(mine))
    def _():
        turn_mid.start()

    normed = norm(middle.astype(jnp.float32))
    loads[5].wait()
    b2_own[...] = dot(squeeze[...], gated(normed, w_ab2, 1, mask_t)).astype(jnp.bfloat16)
    a2[col] = dot(squeeze[...], gated(normed, w_ab2, 0, mask_t)).astype(jnp.bfloat16)
    spread_out(a2.at[col], a2, a2_sems, b2_own, b2, b2_sems)

    for copy in sends[: 2 * (n - 1)]:
        copy.wait_send()

    @pl.when(jnp.logical_not(mine))
    def _():
        turn_pair.wait_send()
        turn_mid.wait_send()
        turn_mid.wait_recv()

    @pl.when(mine)
    def _():
        mid_t[...] = mid_own[...]

    mid_f = dot(spread[...], mid_t[...])
    normed = norm(mid_f)
    right_wide[...] = gated(normed, w_ab2, 1, mask).astype(jnp.float32).reshape(right_wide.shape)
    loads[6].wait()
    gate = sigmoid(dot(normed, w_gate2[...]))
    for copy in sends[2 * (n - 1) :]:
        copy.wait_send()
    total = contract(a2, left_wide, a2_sems, b2, right_wide, b2_sems)
    loads[7].wait()
    updated = finish(mid_f, total, gate, w_proj2)
    out_ref[...] = updated.reshape(side, wide, channels)[:, :side, :]


def on_square(n, pair, res_mask, *weights):
    side, _, channels = pair.shape
    wide = -(-side // 16) * 16
    block = pltpu.VMEM((side * side, channels), jnp.bfloat16)
    blocks = pltpu.VMEM((n, side * side, channels), jnp.bfloat16)
    positions = pltpu.VMEM((side, wide, channels), jnp.float32)
    tile = pltpu.VMEM(pair.shape, pair.dtype)
    sems = pltpu.SemaphoreType.DMA((n,))
    in_hbm = pl.BlockSpec(memory_space=pltpu.HBM)
    return pl.pallas_call(
        functools.partial(kernel, n, side, wide),
        out_shape=pltpu.VMEM(pair.shape, pair.dtype),
        in_specs=[in_hbm] * (2 + len(weights)),
        out_specs=pl.BlockSpec(memory_space=pltpu.VMEM),
        scratch_shapes=[tile, pltpu.SMEM(res_mask.shape, res_mask.dtype)]
        + [pltpu.VMEM(w.shape, w.dtype) for w in weights]
        + [positions] * 3
        + [pltpu.VMEM((side * wide, channels), jnp.float32)] * 2
        + [pltpu.VMEM((side * side, side * wide), jnp.bfloat16)] * 2
        + [pltpu.VMEM((side * wide, side * side), jnp.bfloat16)]
        + [tile, blocks, block, blocks]
        + [block, block, blocks, blocks, block]
        + [pltpu.SemaphoreType.DMA((2 + len(weights),))]
        + [pltpu.SemaphoreType.DMA((2,))] * 2
        + [sems] * 8,
        compiler_params=pltpu.CompilerParams(
            collective_id=0, has_side_effects=True, vmem_limit_bytes=60 * 2**20
        ),
    )(pair, res_mask, *weights)


def solution(mesh):
    n = mesh.shape["rows"]
    square = n == mesh.shape["chan"] * mesh.shape["sub"]

    def per_device(pair, *rest):
        if square and pair.shape[0] == pair.shape[1] and pair.shape[0] <= 16:
            return on_square(n, pair, *rest)
        return on_device(pair, *rest)

    return jax.shard_map(
        per_device,
        mesh=mesh,
        in_specs=(
            P(("groups", "rows"), ("chan", "sub"), None),
            P("groups"),
            P(),
            P(),
            P(),
            P(),
            P(),
            P(),
        ),
        out_specs=P(("groups", "rows"), ("chan", "sub"), None),
        check_vma=False,
    )
```

```python
import functools

import jax
import jax.numpy as jnp
from jax import lax
from jax.experimental import pallas as pl
from jax.experimental.pallas import tpu as pltpu
from jax.sharding import PartitionSpec as P


def normalize(values, axis):
    mean = jnp.mean(values, axis=axis, keepdims=True)
    centered = values - mean
    var = jnp.mean(centered * centered, axis=axis, keepdims=True)
    return centered * lax.rsqrt(var + 1e-05)


def prepare(pair_in, res_mask, w_ab, w_gate):
    row_count = pair_in.shape[0]
    col_count = pair_in.shape[1]
    hidden = w_ab.shape[1] // 4
    pair_f = pair_in.astype(jnp.float32)
    normed = normalize(pair_f, -1).astype(jnp.bfloat16)
    proj = jnp.einsum("ijc,cd->dij", normed, w_ab, preferred_element_type=jnp.float32)
    row_start = lax.axis_index("rows") * row_count
    col_start = lax.axis_index(("chan", "sub")) * col_count
    row_mask = lax.dynamic_slice_in_dim(res_mask, row_start, row_count).astype(jnp.float32)
    col_mask = lax.dynamic_slice_in_dim(res_mask, col_start, col_count).astype(jnp.float32)
    pair_mask = row_mask[:, None] * col_mask[None, :]
    left = (jax.nn.sigmoid(proj[:hidden]) * proj[hidden : 2 * hidden] * pair_mask).astype(
        jnp.bfloat16
    )
    right = (jax.nn.sigmoid(proj[2 * hidden : 3 * hidden]) * proj[3 * hidden :] * pair_mask).astype(
        jnp.bfloat16
    )
    gate = jax.nn.sigmoid(
        jnp.einsum("ijc,ce->ije", normed, w_gate, preferred_element_type=jnp.float32)
    )
    return (pair_f, left, right, gate)


def finish(pair_f, tri_local, gate, w_proj):
    tnorm = normalize(tri_local.astype(jnp.float32), 0).astype(jnp.bfloat16)
    update = jnp.einsum("dij,de->ije", tnorm, w_proj, preferred_element_type=jnp.float32)
    return (pair_f + gate * update).astype(jnp.bfloat16)


def on_device(pair, res_mask, out_ab, out_gate, out_proj, in_ab, in_gate, in_proj):
    pair_f, left, right, gate = prepare(pair, res_mask, out_ab, out_gate)
    left_grp, right_grp = (
        lax.all_to_all(left, ("chan", "sub"), split_axis=0, concat_axis=2, tiled=True),
        lax.all_to_all(right, ("chan", "sub"), split_axis=0, concat_axis=2, tiled=True),
    )
    tri = jnp.einsum(
        "dik,djk->dij",
        left_grp,
        lax.all_gather(right_grp, "rows", axis=1, tiled=True),
        preferred_element_type=jnp.float32,
    ).astype(jnp.bfloat16)
    tri_local = lax.all_to_all(tri, ("chan", "sub"), split_axis=2, concat_axis=0, tiled=True)
    middle = finish(pair_f, tri_local, gate, out_proj)
    mid_f, left, right, gate = prepare(middle, res_mask, in_ab, in_gate)
    left_grp, right_grp = (
        lax.all_to_all(left, ("chan", "sub"), split_axis=0, concat_axis=2, tiled=True),
        lax.all_to_all(right, ("chan", "sub"), split_axis=0, concat_axis=2, tiled=True),
    )
    left_turned = lax.all_to_all(left_grp, "rows", split_axis=2, concat_axis=1, tiled=True)
    tri = jnp.einsum(
        "dki,dkj->dij",
        left_turned,
        lax.all_gather(right_grp, "rows", axis=1, tiled=True),
        preferred_element_type=jnp.float32,
    ).astype(jnp.bfloat16)
    tri_local = lax.all_to_all(tri, ("chan", "sub"), split_axis=2, concat_axis=0, tiled=True)
    return finish(mid_f, tri_local, gate, in_proj)


MESH = pl.DeviceIdType.MESH


def sigmoid(x):
    return 0.5 * jnp.tanh(0.5 * x) + 0.5


def dot(x, y):
    return jnp.dot(x, y, preferred_element_type=jnp.float32)


def turning(side, wide):
    shape = (side * wide, side * wide)
    to = lax.broadcasted_iota(jnp.int32, shape, 0)
    source = lax.broadcasted_iota(jnp.int32, shape, 1)
    q, p = to // wide, to % wide
    hit = (source == p * wide + q) & (p < side)
    return jnp.where(hit, 1.0, 0.0).astype(jnp.bfloat16)


def kernel(
    n,
    side,
    wide,
    pair_hbm,
    mask_hbm,
    w_ab1_hbm,
    w_gate1_hbm,
    w_proj1_hbm,
    w_ab2_hbm,
    w_gate2_hbm,
    w_proj2_hbm,
    out_ref,
    pair_v,
    mask_ref,
    w_ab1,
    w_gate1,
    w_proj1,
    w_ab2,
    w_gate2,
    w_proj2,
    padded,
    left_wide,
    right_wide,
    mask,
    mask_t,
    turn,
    pair_t,
    a1,
    a1_own,
    b1,
    mid_t,
    mid_own,
    a2,
    b2,
    b2_own,
    in_sem,
    t_send,
    t_recv,
    a1_send,
    a1_recv,
    b1_send,
    b1_recv,
    a2_send,
    a2_recv,
    b2_send,
    b2_recv,
):
    row = lax.axis_index("rows")
    subs = lax.axis_size("sub")
    col = lax.axis_index("chan") * subs + lax.axis_index("sub")
    mine = row == col
    channels = pair_hbm.shape[-1]

    def device(r, c):
        return {"rows": r, "chan": c // subs, "sub": c % subs}

    barrier = pltpu.get_barrier_semaphore()
    for step in range(1, n):
        pl.semaphore_signal(
            barrier, inc=1, device_id=device(col, (row + step) % n), device_id_type=MESH
        )
    for step in range(1, n):
        pl.semaphore_signal(
            barrier, inc=1, device_id=device(row, (col + step) % n), device_id_type=MESH
        )

    @pl.when(jnp.logical_not(mine))
    def _():
        pl.semaphore_signal(barrier, inc=1, device_id=device(col, row), device_id_type=MESH)

    loads = []
    for place, (src, dst) in enumerate(
        (
            (pair_hbm, pair_v),
            (mask_hbm, mask_ref),
            (w_ab1_hbm, w_ab1),
            (w_gate1_hbm, w_gate1),
            (w_proj1_hbm, w_proj1),
            (w_ab2_hbm, w_ab2),
            (w_gate2_hbm, w_gate2),
            (w_proj2_hbm, w_proj2),
        )
    ):
        load = pltpu.make_async_copy(src, dst, in_sem.at[place])
        load.start()
        loads.append(load)

    turn[...] = turning(side, wide)

    def tile_mask(rows, cols):
        sublane = lax.broadcasted_iota(jnp.int32, (wide, channels), 0)
        col_mask = jnp.zeros((wide, channels), jnp.float32)
        for j in range(side):
            value = mask_ref[cols * side + j].astype(jnp.float32)
            col_mask = jnp.where(sublane == j, value, col_mask)
        return jnp.concatenate(
            [col_mask * mask_ref[rows * side + i].astype(jnp.float32) for i in range(side)],
            axis=0,
        )

    def widen(block):
        padded[:, :side, :] = block[...].astype(jnp.float32)
        return padded[...].reshape(side * wide, channels)

    def norm(values):
        return normalize(values, -1).astype(jnp.bfloat16)

    def gated(normed, w_ab, half, mask):
        hidden = w_ab.shape[1] // 4
        proj = dot(normed, w_ab[:, 2 * half * hidden : 2 * (half + 1) * hidden])
        return (sigmoid(proj[:, :hidden]) * proj[:, hidden:] * mask[...]).astype(jnp.bfloat16)

    def finish(values, total, gate, w_proj):
        tri = jnp.concatenate(total, axis=0).astype(jnp.bfloat16).astype(jnp.float32)
        return (values + gate * dot(norm(tri), w_proj[...])).astype(jnp.bfloat16)

    def send(src, dst, send_sem, recv_sem, r, c):
        return pltpu.make_async_remote_copy(
            src_ref=src,
            dst_ref=dst,
            send_sem=send_sem,
            recv_sem=recv_sem,
            device_id=device(r, c),
            device_id_type=MESH,
        )

    sends = []

    def spread_out(along, along_buf, along_sems, turn, turn_buf, turn_sems):
        for s in range(1, n):
            copy = send(
                turn, turn_buf.at[col], turn_sems[0].at[s], turn_sems[1].at[col], (col + s) % n, row
            )
            copy.start()
            sends.append(copy)
        for s in range(1, n):
            copy = send(
                along, along_buf.at[col], along_sems[0].at[s], along_sems[1].at[col], row, (col + s) % n
            )
            copy.start()
            sends.append(copy)

    def await_block(buf, slot, sems):
        send(buf.at[slot], buf.at[slot], sems[0].at[0], sems[1].at[slot], row, col).wait_recv()

    def widen_block(dst, block):
        dst[...] = block[...].astype(jnp.float32).reshape(dst.shape)

    def add_products(total):
        def step(k, total):
            row_of_right = right_wide[k]
            return tuple(
                total[i] + left_wide[k, pl.ds(i, 1), :] * row_of_right for i in range(side)
            )

        return lax.fori_loop(0, side, step, total, unroll=True)

    def zeros():
        return tuple(jnp.zeros((wide, channels), jnp.float32) for _ in range(side))

    def contract(along, along_wide, along_sems, turn, turn_wide, turn_sems):
        total = zeros()
        for s in range(n):
            block = (row + s) % n
            if s:
                await_block(turn, block, turn_sems)
                widen_block(turn_wide, turn.at[block])

            @pl.when(block != col)
            def _():
                await_block(along, block, along_sems)

            widen_block(along_wide, along.at[block])
            total = add_products(total)
        return total

    a1_sems, b1_sems = (a1_send, a1_recv), (b1_send, b1_recv)
    a2_sems, b2_sems = (a2_send, a2_recv), (b2_send, b2_recv)
    padded[...] = jnp.zeros_like(padded)
    loads[0].wait()
    pair_f = widen(pair_v)
    normed = norm(pair_f)
    loads[1].wait()
    mask[...] = tile_mask(row, col)
    mask_t[...] = tile_mask(col, row)
    loads[2].wait()
    left = gated(normed, w_ab1, 0, mask)
    right = gated(normed, w_ab1, 1, mask)
    a1_own[...] = dot(turn[...], left).astype(jnp.bfloat16)
    b1[col] = dot(turn[...], right).astype(jnp.bfloat16)

    @pl.when(mine)
    def _():
        pl.semaphore_wait(barrier, 2 * (n - 1))

    @pl.when(jnp.logical_not(mine))
    def _():
        pl.semaphore_wait(barrier, 2 * n - 1)

    turn_pair = send(pair_hbm, pair_t, t_send.at[0], t_recv.at[0], col, row)
    stay_pair = pltpu.make_async_copy(pair_hbm, pair_t, t_send.at[0])

    @pl.when(jnp.logical_not(mine))
    def _():
        turn_pair.start()

    @pl.when(mine)
    def _():
        stay_pair.start()

    spread_out(b1.at[col], b1, b1_sems, a1_own, a1, a1_sems)

    @pl.when(jnp.logical_not(mine))
    def _():
        turn_pair.wait_recv()

    @pl.when(mine)
    def _():
        stay_pair.wait()

    pair_f = widen(pair_t)
    normed = norm(pair_f)
    left_wide[...] = dot(turn[...], gated(normed, w_ab1, 0, mask_t)).reshape(left_wide.shape)
    loads[3].wait()
    gate = sigmoid(dot(normed, w_gate1[...]))
    total = contract(b1, right_wide, b1_sems, a1, left_wide, a1_sems)
    loads[4].wait()
    middle = finish(pair_f, total, gate, w_proj1)

    mid_own[...] = middle
    turn_mid = send(mid_own, mid_t, t_send.at[1], t_recv.at[1], col, row)

    @pl.when(jnp.logical_not(mine))
    def _():
        turn_mid.start()

    normed = norm(middle.astype(jnp.float32))
    loads[5].wait()
    b2_own[...] = gated(normed, w_ab2, 1, mask_t)
    a2[col] = gated(normed, w_ab2, 0, mask_t)
    spread_out(a2.at[col], a2, a2_sems, b2_own, b2, b2_sems)

    for copy in sends[: 2 * (n - 1)]:
        copy.wait_send()

    @pl.when(jnp.logical_not(mine))
    def _():
        turn_pair.wait_send()
        turn_mid.wait_send()
        turn_mid.wait_recv()

    @pl.when(mine)
    def _():
        mid_t[...] = mid_own[...]

    mid_f = mid_t[...].astype(jnp.float32)
    normed = norm(mid_f)
    right_wide[...] = gated(normed, w_ab2, 1, mask).astype(jnp.float32).reshape(right_wide.shape)
    loads[6].wait()
    gate = sigmoid(dot(normed, w_gate2[...]))
    for copy in sends[2 * (n - 1) :]:
        copy.wait_send()
    total = contract(a2, left_wide, a2_sems, b2, right_wide, b2_sems)
    loads[7].wait()
    updated = finish(mid_f, total, gate, w_proj2)
    out_ref[...] = updated.reshape(side, wide, channels)[:, :side, :]


def on_square(n, pair, res_mask, *weights):
    side, _, channels = pair.shape
    wide = -(-side // 16) * 16
    block = pltpu.VMEM((side * wide, channels), jnp.bfloat16)
    blocks = pltpu.VMEM((n, side * wide, channels), jnp.bfloat16)
    positions = pltpu.VMEM((side, wide, channels), jnp.float32)
    tile = pltpu.VMEM(pair.shape, pair.dtype)
    sems = pltpu.SemaphoreType.DMA((n,))
    in_hbm = pl.BlockSpec(memory_space=pltpu.HBM)
    return pl.pallas_call(
        functools.partial(kernel, n, side, wide),
        out_shape=pltpu.VMEM(pair.shape, pair.dtype),
        in_specs=[in_hbm] * (2 + len(weights)),
        out_specs=pl.BlockSpec(memory_space=pltpu.VMEM),
        scratch_shapes=[tile, pltpu.SMEM(res_mask.shape, res_mask.dtype)]
        + [pltpu.VMEM(w.shape, w.dtype) for w in weights]
        + [positions] * 3
        + [pltpu.VMEM((side * wide, channels), jnp.float32)] * 2
        + [pltpu.VMEM((side * wide, side * wide), jnp.bfloat16)]
        + [tile, blocks, block, blocks]
        + [block, block, blocks, blocks, block]
        + [pltpu.SemaphoreType.DMA((2 + len(weights),))]
        + [pltpu.SemaphoreType.DMA((2,))] * 2
        + [sems] * 8,
        compiler_params=pltpu.CompilerParams(
            collective_id=0, has_side_effects=True, vmem_limit_bytes=60 * 2**20
        ),
    )(pair, res_mask, *weights)


def solution(mesh):
    n = mesh.shape["rows"]
    square = n == mesh.shape["chan"] * mesh.shape["sub"]

    def per_device(pair, *rest):
        if square and pair.shape[0] == pair.shape[1] and pair.shape[0] <= 16:
            return on_square(n, pair, *rest)
        return on_device(pair, *rest)

    return jax.shard_map(
        per_device,
        mesh=mesh,
        in_specs=(
            P(("groups", "rows"), ("chan", "sub"), None),
            P("groups"),
            P(),
            P(),
            P(),
            P(),
            P(),
            P(),
        ),
        out_specs=P(("groups", "rows"), ("chan", "sub"), None),
        check_vma=False,
    )
```

```python
import functools

import jax
import jax.numpy as jnp
from jax import lax
from jax.experimental import pallas as pl
from jax.experimental.pallas import tpu as pltpu
from jax.sharding import PartitionSpec as P


def normalize(values, axis):
    mean = jnp.mean(values, axis=axis, keepdims=True)
    centered = values - mean
    var = jnp.mean(centered * centered, axis=axis, keepdims=True)
    return centered * lax.rsqrt(var + 1e-05)


def prepare(pair_in, res_mask, w_ab, w_gate):
    row_count = pair_in.shape[0]
    col_count = pair_in.shape[1]
    hidden = w_ab.shape[1] // 4
    pair_f = pair_in.astype(jnp.float32)
    normed = normalize(pair_f, -1).astype(jnp.bfloat16)
    proj = jnp.einsum("ijc,cd->dij", normed, w_ab, preferred_element_type=jnp.float32)
    row_start = lax.axis_index("rows") * row_count
    col_start = lax.axis_index(("chan", "sub")) * col_count
    row_mask = lax.dynamic_slice_in_dim(res_mask, row_start, row_count).astype(jnp.float32)
    col_mask = lax.dynamic_slice_in_dim(res_mask, col_start, col_count).astype(jnp.float32)
    pair_mask = row_mask[:, None] * col_mask[None, :]
    left = (jax.nn.sigmoid(proj[:hidden]) * proj[hidden : 2 * hidden] * pair_mask).astype(
        jnp.bfloat16
    )
    right = (jax.nn.sigmoid(proj[2 * hidden : 3 * hidden]) * proj[3 * hidden :] * pair_mask).astype(
        jnp.bfloat16
    )
    gate = jax.nn.sigmoid(
        jnp.einsum("ijc,ce->ije", normed, w_gate, preferred_element_type=jnp.float32)
    )
    return (pair_f, left, right, gate)


def finish(pair_f, tri_local, gate, w_proj):
    tnorm = normalize(tri_local.astype(jnp.float32), 0).astype(jnp.bfloat16)
    update = jnp.einsum("dij,de->ije", tnorm, w_proj, preferred_element_type=jnp.float32)
    return (pair_f + gate * update).astype(jnp.bfloat16)


def on_device(pair, res_mask, out_ab, out_gate, out_proj, in_ab, in_gate, in_proj):
    pair_f, left, right, gate = prepare(pair, res_mask, out_ab, out_gate)
    left_grp, right_grp = (
        lax.all_to_all(left, ("chan", "sub"), split_axis=0, concat_axis=2, tiled=True),
        lax.all_to_all(right, ("chan", "sub"), split_axis=0, concat_axis=2, tiled=True),
    )
    tri = jnp.einsum(
        "dik,djk->dij",
        left_grp,
        lax.all_gather(right_grp, "rows", axis=1, tiled=True),
        preferred_element_type=jnp.float32,
    ).astype(jnp.bfloat16)
    tri_local = lax.all_to_all(tri, ("chan", "sub"), split_axis=2, concat_axis=0, tiled=True)
    middle = finish(pair_f, tri_local, gate, out_proj)
    mid_f, left, right, gate = prepare(middle, res_mask, in_ab, in_gate)
    left_grp, right_grp = (
        lax.all_to_all(left, ("chan", "sub"), split_axis=0, concat_axis=2, tiled=True),
        lax.all_to_all(right, ("chan", "sub"), split_axis=0, concat_axis=2, tiled=True),
    )
    left_turned = lax.all_to_all(left_grp, "rows", split_axis=2, concat_axis=1, tiled=True)
    tri = jnp.einsum(
        "dki,dkj->dij",
        left_turned,
        lax.all_gather(right_grp, "rows", axis=1, tiled=True),
        preferred_element_type=jnp.float32,
    ).astype(jnp.bfloat16)
    tri_local = lax.all_to_all(tri, ("chan", "sub"), split_axis=2, concat_axis=0, tiled=True)
    return finish(mid_f, tri_local, gate, in_proj)


MESH = pl.DeviceIdType.MESH


def sigmoid(x):
    return 0.5 * jnp.tanh(0.5 * x) + 0.5


def dot(x, y):
    return jnp.dot(x, y, preferred_element_type=jnp.float32)


def turning(side, wide):
    shape = (side * wide, side * wide)
    to = lax.broadcasted_iota(jnp.int32, shape, 0)
    source = lax.broadcasted_iota(jnp.int32, shape, 1)
    q, p = to // wide, to % wide
    hit = (source == p * wide + q) & (p < side)
    return jnp.where(hit, 1.0, 0.0).astype(jnp.bfloat16)


def kernel(
    n,
    side,
    wide,
    pair_hbm,
    mask_hbm,
    w_ab1_hbm,
    w_gate1_hbm,
    w_proj1_hbm,
    w_ab2_hbm,
    w_gate2_hbm,
    w_proj2_hbm,
    out_ref,
    pair_v,
    mask_ref,
    w_ab1,
    w_gate1,
    w_proj1,
    w_ab2,
    w_gate2,
    w_proj2,
    padded,
    left_wide,
    right_wide,
    mask,
    mask_t,
    turn,
    pair_t,
    a1,
    a1_own,
    b1,
    mid_t,
    mid_own,
    a2,
    b2,
    b2_own,
    in_sem,
    t_send,
    t_recv,
    a1_send,
    a1_recv,
    b1_send,
    b1_recv,
    a2_send,
    a2_recv,
    b2_send,
    b2_recv,
):
    row = lax.axis_index("rows")
    subs = lax.axis_size("sub")
    col = lax.axis_index("chan") * subs + lax.axis_index("sub")
    mine = row == col
    channels = pair_hbm.shape[-1]

    def device(r, c):
        return {"rows": r, "chan": c // subs, "sub": c % subs}

    barrier = pltpu.get_barrier_semaphore()
    for step in range(1, n):
        pl.semaphore_signal(
            barrier, inc=1, device_id=device(col, (row + step) % n), device_id_type=MESH
        )
    for step in range(1, n):
        pl.semaphore_signal(
            barrier, inc=1, device_id=device(row, (col + step) % n), device_id_type=MESH
        )

    @pl.when(jnp.logical_not(mine))
    def _():
        pl.semaphore_signal(barrier, inc=1, device_id=device(col, row), device_id_type=MESH)

    loads = []
    for place, (src, dst) in enumerate(
        (
            (pair_hbm, pair_v),
            (mask_hbm, mask_ref),
            (w_ab1_hbm, w_ab1),
            (w_gate1_hbm, w_gate1),
            (w_proj1_hbm, w_proj1),
            (w_ab2_hbm, w_ab2),
            (w_gate2_hbm, w_gate2),
            (w_proj2_hbm, w_proj2),
        )
    ):
        load = pltpu.make_async_copy(src, dst, in_sem.at[place])
        load.start()
        loads.append(load)

    turn[...] = turning(side, wide)

    def tile_mask(rows, cols):
        sublane = lax.broadcasted_iota(jnp.int32, (wide, channels), 0)
        col_mask = jnp.zeros((wide, channels), jnp.float32)
        for j in range(side):
            value = mask_ref[cols * side + j].astype(jnp.float32)
            col_mask = jnp.where(sublane == j, value, col_mask)
        return jnp.concatenate(
            [col_mask * mask_ref[rows * side + i].astype(jnp.float32) for i in range(side)],
            axis=0,
        )

    def widen(block):
        padded[:, :side, :] = block[...].astype(jnp.float32)
        return padded[...].reshape(side * wide, channels)

    def norm(values):
        return normalize(values, -1).astype(jnp.bfloat16)

    def gated(normed, w_ab, half, mask):
        hidden = w_ab.shape[1] // 4
        proj = dot(normed, w_ab[:, 2 * half * hidden : 2 * (half + 1) * hidden])
        return (sigmoid(proj[:, :hidden]) * proj[:, hidden:] * mask[...]).astype(jnp.bfloat16)

    def finish(values, total, gate, w_proj):
        tri = jnp.concatenate(total, axis=0).astype(jnp.bfloat16).astype(jnp.float32)
        return (values + gate * dot(norm(tri), w_proj[...])).astype(jnp.bfloat16)

    def send(src, dst, send_sem, recv_sem, r, c):
        return pltpu.make_async_remote_copy(
            src_ref=src,
            dst_ref=dst,
            send_sem=send_sem,
            recv_sem=recv_sem,
            device_id=device(r, c),
            device_id_type=MESH,
        )

    sends = []

    half = side - 8
    first = lax.broadcasted_iota(jnp.int32, (8, channels), 0) < half

    def pack(x):
        parts = [x[p * wide : p * wide + 8] for p in range(side)]
        for p in range(0, side, 2):
            odd = pltpu.roll(x[(p + 1) * wide + 8 : (p + 2) * wide], half, 0)
            parts.append(jnp.where(first, x[p * wide + 8 : (p + 1) * wide], odd))
        return jnp.concatenate(parts, axis=0).astype(jnp.bfloat16)

    def spread_out(along, along_buf, along_sems, turn, turn_buf, turn_sems):
        for s in range(1, n):
            copy = send(
                turn, turn_buf.at[col], turn_sems[0].at[s], turn_sems[1].at[col], (col + s) % n, row
            )
            copy.start()
            sends.append(copy)
        for s in range(1, n):
            copy = send(
                along, along_buf.at[col], along_sems[0].at[s], along_sems[1].at[col], row, (col + s) % n
            )
            copy.start()
            sends.append(copy)

    def await_block(buf, slot, sems):
        send(buf.at[slot], buf.at[slot], sems[0].at[0], sems[1].at[slot], row, col).wait_recv()

    def widen_block(dst, block):
        x = block[...].astype(jnp.float32)
        for p in range(side):
            dst[p, :8, :] = x[8 * p : 8 * (p + 1)]
        for p in range(0, side, 2):
            rest = x[8 * side + 4 * p : 8 * side + 4 * p + 8]
            dst[p, 8:, :] = rest
            dst[p + 1, 8:, :] = pltpu.roll(rest, half, 0)

    def add_products(total):
        def step(k, total):
            row_of_right = right_wide[k]
            return tuple(
                total[i] + left_wide[k, pl.ds(i, 1), :] * row_of_right for i in range(side)
            )

        return lax.fori_loop(0, side, step, total, unroll=True)

    def zeros():
        return tuple(jnp.zeros((wide, channels), jnp.float32) for _ in range(side))

    def contract(along, along_wide, along_sems, turn, turn_wide, turn_sems):
        total = zeros()
        for s in range(n):
            block = (row + s) % n
            if s:
                await_block(turn, block, turn_sems)
                widen_block(turn_wide, turn.at[block])

            @pl.when(block != col)
            def _():
                await_block(along, block, along_sems)

            widen_block(along_wide, along.at[block])
            total = add_products(total)
        return total

    a1_sems, b1_sems = (a1_send, a1_recv), (b1_send, b1_recv)
    a2_sems, b2_sems = (a2_send, a2_recv), (b2_send, b2_recv)
    padded[...] = jnp.zeros_like(padded)
    loads[0].wait()
    pair_f = widen(pair_v)
    normed = norm(pair_f)
    loads[1].wait()
    mask[...] = tile_mask(row, col)
    mask_t[...] = tile_mask(col, row)
    loads[2].wait()
    left = gated(normed, w_ab1, 0, mask)
    right = gated(normed, w_ab1, 1, mask)
    a1_own[...] = pack(dot(turn[...], left))
    b1[col] = pack(dot(turn[...], right))

    @pl.when(mine)
    def _():
        pl.semaphore_wait(barrier, 2 * (n - 1))

    @pl.when(jnp.logical_not(mine))
    def _():
        pl.semaphore_wait(barrier, 2 * n - 1)

    turn_pair = send(pair_hbm, pair_t, t_send.at[0], t_recv.at[0], col, row)
    stay_pair = pltpu.make_async_copy(pair_hbm, pair_t, t_send.at[0])

    @pl.when(jnp.logical_not(mine))
    def _():
        turn_pair.start()

    @pl.when(mine)
    def _():
        stay_pair.start()

    spread_out(b1.at[col], b1, b1_sems, a1_own, a1, a1_sems)

    @pl.when(jnp.logical_not(mine))
    def _():
        turn_pair.wait_recv()

    @pl.when(mine)
    def _():
        stay_pair.wait()

    pair_f = widen(pair_t)
    normed = norm(pair_f)
    left_wide[...] = dot(turn[...], gated(normed, w_ab1, 0, mask_t)).reshape(left_wide.shape)
    loads[3].wait()
    gate = sigmoid(dot(normed, w_gate1[...]))
    total = contract(b1, right_wide, b1_sems, a1, left_wide, a1_sems)
    loads[4].wait()
    middle = finish(pair_f, total, gate, w_proj1)

    mid_own[...] = pack(middle.astype(jnp.float32))
    turn_mid = send(mid_own, mid_t, t_send.at[1], t_recv.at[1], col, row)

    @pl.when(jnp.logical_not(mine))
    def _():
        turn_mid.start()

    normed = norm(middle.astype(jnp.float32))
    loads[5].wait()
    b2_own[...] = pack(gated(normed, w_ab2, 1, mask_t).astype(jnp.float32))
    a2[col] = pack(gated(normed, w_ab2, 0, mask_t).astype(jnp.float32))
    spread_out(a2.at[col], a2, a2_sems, b2_own, b2, b2_sems)

    for copy in sends[: 2 * (n - 1)]:
        copy.wait_send()

    @pl.when(jnp.logical_not(mine))
    def _():
        turn_pair.wait_send()
        turn_mid.wait_send()
        turn_mid.wait_recv()

    @pl.when(mine)
    def _():
        mid_t[...] = mid_own[...]

    widen_block(padded, mid_t)
    mid_f = padded[...].reshape(side * wide, channels)
    normed = norm(mid_f)
    right_wide[...] = gated(normed, w_ab2, 1, mask).astype(jnp.float32).reshape(right_wide.shape)
    loads[6].wait()
    gate = sigmoid(dot(normed, w_gate2[...]))
    for copy in sends[2 * (n - 1) :]:
        copy.wait_send()
    total = contract(a2, left_wide, a2_sems, b2, right_wide, b2_sems)
    loads[7].wait()
    updated = finish(mid_f, total, gate, w_proj2)
    out_ref[...] = updated.reshape(side, wide, channels)[:, :side, :]


def on_square(n, pair, res_mask, *weights):
    side, _, channels = pair.shape
    wide = -(-side // 16) * 16
    block = pltpu.VMEM((side * side, channels), jnp.bfloat16)
    blocks = pltpu.VMEM((n, side * side, channels), jnp.bfloat16)
    positions = pltpu.VMEM((side, wide, channels), jnp.float32)
    tile = pltpu.VMEM(pair.shape, pair.dtype)
    sems = pltpu.SemaphoreType.DMA((n,))
    in_hbm = pl.BlockSpec(memory_space=pltpu.HBM)
    return pl.pallas_call(
        functools.partial(kernel, n, side, wide),
        out_shape=pltpu.VMEM(pair.shape, pair.dtype),
        in_specs=[in_hbm] * (2 + len(weights)),
        out_specs=pl.BlockSpec(memory_space=pltpu.VMEM),
        scratch_shapes=[tile, pltpu.SMEM(res_mask.shape, res_mask.dtype)]
        + [pltpu.VMEM(w.shape, w.dtype) for w in weights]
        + [positions] * 3
        + [pltpu.VMEM((side * wide, channels), jnp.float32)] * 2
        + [pltpu.VMEM((side * wide, side * wide), jnp.bfloat16)]
        + [tile, blocks, block, blocks]
        + [block, block, blocks, blocks, block]
        + [pltpu.SemaphoreType.DMA((2 + len(weights),))]
        + [pltpu.SemaphoreType.DMA((2,))] * 2
        + [sems] * 8,
        compiler_params=pltpu.CompilerParams(
            collective_id=0, has_side_effects=True, vmem_limit_bytes=60 * 2**20
        ),
    )(pair, res_mask, *weights)


def solution(mesh):
    n = mesh.shape["rows"]
    square = n == mesh.shape["chan"] * mesh.shape["sub"]

    def per_device(pair, *rest):
        if square and pair.shape[0] == pair.shape[1] == 12:
            return on_square(n, pair, *rest)
        return on_device(pair, *rest)

    return jax.shard_map(
        per_device,
        mesh=mesh,
        in_specs=(
            P(("groups", "rows"), ("chan", "sub"), None),
            P("groups"),
            P(),
            P(),
            P(),
            P(),
            P(),
            P(),
        ),
        out_specs=P(("groups", "rows"), ("chan", "sub"), None),
        check_vma=False,
    )
```

```python
import functools

import jax
import jax.numpy as jnp
from jax import lax
from jax.experimental import pallas as pl
from jax.experimental.pallas import tpu as pltpu
from jax.sharding import PartitionSpec as P


def normalize(values, axis):
    mean = jnp.mean(values, axis=axis, keepdims=True)
    centered = values - mean
    var = jnp.mean(centered * centered, axis=axis, keepdims=True)
    return centered * lax.rsqrt(var + 1e-05)


def prepare(pair_in, res_mask, w_ab, w_gate):
    row_count = pair_in.shape[0]
    col_count = pair_in.shape[1]
    hidden = w_ab.shape[1] // 4
    pair_f = pair_in.astype(jnp.float32)
    normed = normalize(pair_f, -1).astype(jnp.bfloat16)
    proj = jnp.einsum("ijc,cd->dij", normed, w_ab, preferred_element_type=jnp.float32)
    row_start = lax.axis_index("rows") * row_count
    col_start = lax.axis_index(("chan", "sub")) * col_count
    row_mask = lax.dynamic_slice_in_dim(res_mask, row_start, row_count).astype(jnp.float32)
    col_mask = lax.dynamic_slice_in_dim(res_mask, col_start, col_count).astype(jnp.float32)
    pair_mask = row_mask[:, None] * col_mask[None, :]
    left = (jax.nn.sigmoid(proj[:hidden]) * proj[hidden : 2 * hidden] * pair_mask).astype(
        jnp.bfloat16
    )
    right = (jax.nn.sigmoid(proj[2 * hidden : 3 * hidden]) * proj[3 * hidden :] * pair_mask).astype(
        jnp.bfloat16
    )
    gate = jax.nn.sigmoid(
        jnp.einsum("ijc,ce->ije", normed, w_gate, preferred_element_type=jnp.float32)
    )
    return (pair_f, left, right, gate)


def finish(pair_f, tri_local, gate, w_proj):
    tnorm = normalize(tri_local.astype(jnp.float32), 0).astype(jnp.bfloat16)
    update = jnp.einsum("dij,de->ije", tnorm, w_proj, preferred_element_type=jnp.float32)
    return (pair_f + gate * update).astype(jnp.bfloat16)


def on_device(pair, res_mask, out_ab, out_gate, out_proj, in_ab, in_gate, in_proj):
    pair_f, left, right, gate = prepare(pair, res_mask, out_ab, out_gate)
    left_grp, right_grp = (
        lax.all_to_all(left, ("chan", "sub"), split_axis=0, concat_axis=2, tiled=True),
        lax.all_to_all(right, ("chan", "sub"), split_axis=0, concat_axis=2, tiled=True),
    )
    tri = jnp.einsum(
        "dik,djk->dij",
        left_grp,
        lax.all_gather(right_grp, "rows", axis=1, tiled=True),
        preferred_element_type=jnp.float32,
    ).astype(jnp.bfloat16)
    tri_local = lax.all_to_all(tri, ("chan", "sub"), split_axis=2, concat_axis=0, tiled=True)
    middle = finish(pair_f, tri_local, gate, out_proj)
    mid_f, left, right, gate = prepare(middle, res_mask, in_ab, in_gate)
    left_grp, right_grp = (
        lax.all_to_all(left, ("chan", "sub"), split_axis=0, concat_axis=2, tiled=True),
        lax.all_to_all(right, ("chan", "sub"), split_axis=0, concat_axis=2, tiled=True),
    )
    left_turned = lax.all_to_all(left_grp, "rows", split_axis=2, concat_axis=1, tiled=True)
    tri = jnp.einsum(
        "dki,dkj->dij",
        left_turned,
        lax.all_gather(right_grp, "rows", axis=1, tiled=True),
        preferred_element_type=jnp.float32,
    ).astype(jnp.bfloat16)
    tri_local = lax.all_to_all(tri, ("chan", "sub"), split_axis=2, concat_axis=0, tiled=True)
    return finish(mid_f, tri_local, gate, in_proj)


MESH = pl.DeviceIdType.MESH


def sigmoid(x):
    return 0.5 * jnp.tanh(0.5 * x) + 0.5


def dot(x, y):
    return jnp.dot(x, y, preferred_element_type=jnp.float32)


def turning(side, wide):
    shape = (side * wide, side * wide)
    to = lax.broadcasted_iota(jnp.int32, shape, 0)
    source = lax.broadcasted_iota(jnp.int32, shape, 1)
    q, p = to // wide, to % wide
    hit = (source == p * wide + q) & (p < side)
    return jnp.where(hit, 1.0, 0.0).astype(jnp.bfloat16)


def kernel(
    n,
    side,
    wide,
    pair_hbm,
    mask_hbm,
    w_ab1_hbm,
    w_gate1_hbm,
    w_proj1_hbm,
    w_ab2_hbm,
    w_gate2_hbm,
    w_proj2_hbm,
    out_ref,
    pair_v,
    mask_ref,
    w_ab1,
    w_gate1,
    w_proj1,
    w_ab2,
    w_gate2,
    w_proj2,
    padded,
    left_wide,
    right_wide,
    mask,
    mask_t,
    turn,
    pair_t,
    a1,
    a1_own,
    b1,
    mid_t,
    mid_own,
    a2,
    b2,
    b2_own,
    in_sem,
    t_send,
    t_recv,
    a1_send,
    a1_recv,
    b1_send,
    b1_recv,
    a2_send,
    a2_recv,
    b2_send,
    b2_recv,
):
    row = lax.axis_index("rows")
    subs = lax.axis_size("sub")
    col = lax.axis_index("chan") * subs + lax.axis_index("sub")
    mine = row == col
    channels = pair_hbm.shape[-1]

    def device(r, c):
        return {"rows": r, "chan": c // subs, "sub": c % subs}

    barrier = pltpu.get_barrier_semaphore()
    for step in range(1, n):
        pl.semaphore_signal(
            barrier, inc=1, device_id=device(col, (row + step) % n), device_id_type=MESH
        )
    for step in range(1, n):
        pl.semaphore_signal(
            barrier, inc=1, device_id=device(row, (col + step) % n), device_id_type=MESH
        )

    @pl.when(jnp.logical_not(mine))
    def _():
        pl.semaphore_signal(barrier, inc=1, device_id=device(col, row), device_id_type=MESH)

    loads = []
    for place, (src, dst) in enumerate(
        (
            (pair_hbm, pair_v),
            (mask_hbm, mask_ref),
            (w_ab1_hbm, w_ab1),
            (w_gate1_hbm, w_gate1),
            (w_proj1_hbm, w_proj1),
            (w_ab2_hbm, w_ab2),
            (w_gate2_hbm, w_gate2),
            (w_proj2_hbm, w_proj2),
        )
    ):
        load = pltpu.make_async_copy(src, dst, in_sem.at[place])
        load.start()
        loads.append(load)

    turn[...] = turning(side, wide)

    def tile_mask(rows, cols):
        sublane = lax.broadcasted_iota(jnp.int32, (wide, channels), 0)
        col_mask = jnp.zeros((wide, channels), jnp.float32)
        for j in range(side):
            value = mask_ref[cols * side + j].astype(jnp.float32)
            col_mask = jnp.where(sublane == j, value, col_mask)
        return jnp.concatenate(
            [col_mask * mask_ref[rows * side + i].astype(jnp.float32) for i in range(side)],
            axis=0,
        )

    def widen(block):
        padded[:, :side, :] = block[...].astype(jnp.float32)
        return padded[...].reshape(side * wide, channels)

    def norm(values):
        return normalize(values, -1).astype(jnp.bfloat16)

    def gated(normed, w_ab, half, mask):
        hidden = w_ab.shape[1] // 4
        proj = dot(normed, w_ab[:, 2 * half * hidden : 2 * (half + 1) * hidden])
        return (sigmoid(proj[:, :hidden]) * proj[:, hidden:] * mask[...]).astype(jnp.bfloat16)

    def finish(values, total, gate, w_proj):
        tri = jnp.concatenate(total, axis=0).astype(jnp.bfloat16).astype(jnp.float32)
        return (values + gate * dot(norm(tri), w_proj[...])).astype(jnp.bfloat16)

    def send(src, dst, send_sem, recv_sem, r, c):
        return pltpu.make_async_remote_copy(
            src_ref=src,
            dst_ref=dst,
            send_sem=send_sem,
            recv_sem=recv_sem,
            device_id=device(r, c),
            device_id_type=MESH,
        )

    sends = []

    half = side - 8
    first = lax.broadcasted_iota(jnp.int32, (8, channels), 0) < half

    def pack(x):
        parts = [x[p * wide : p * wide + 8] for p in range(side)]
        for p in range(0, side, 2):
            odd = pltpu.roll(x[(p + 1) * wide + 8 : (p + 2) * wide], half, 0)
            parts.append(jnp.where(first, x[p * wide + 8 : (p + 1) * wide], odd))
        return jnp.concatenate(parts, axis=0).astype(jnp.bfloat16)

    def spread_turned(turn, turn_buf, turn_sems):
        for s in range(1, n):
            copy = send(
                turn, turn_buf.at[col], turn_sems[0].at[s], turn_sems[1].at[col], (col + s) % n, row
            )
            copy.start()
            sends.append(copy)

    def spread_along(along, along_buf, along_sems):
        for s in range(1, n):
            copy = send(
                along, along_buf.at[col], along_sems[0].at[s], along_sems[1].at[col], row, (col + s) % n
            )
            copy.start()
            sends.append(copy)

    def await_block(buf, slot, sems):
        send(buf.at[slot], buf.at[slot], sems[0].at[0], sems[1].at[slot], row, col).wait_recv()

    def widen_block(dst, block):
        x = block[...].astype(jnp.float32)
        for p in range(side):
            dst[p, :8, :] = x[8 * p : 8 * (p + 1)]
        for p in range(0, side, 2):
            rest = x[8 * side + 4 * p : 8 * side + 4 * p + 8]
            dst[p, 8:, :] = rest
            dst[p + 1, 8:, :] = pltpu.roll(rest, half, 0)

    def add_products(total):
        def step(k, total):
            row_of_right = right_wide[k]
            return tuple(
                total[i] + left_wide[k, pl.ds(i, 1), :] * row_of_right for i in range(side)
            )

        return lax.fori_loop(0, side, step, total, unroll=True)

    def zeros():
        return tuple(jnp.zeros((wide, channels), jnp.float32) for _ in range(side))

    def contract(along, along_wide, along_sems, turn, turn_wide, turn_sems):
        total = zeros()
        for s in range(n):
            block = (row + s) % n
            if s:
                await_block(turn, block, turn_sems)
                widen_block(turn_wide, turn.at[block])

            @pl.when(block != col)
            def _():
                await_block(along, block, along_sems)

            widen_block(along_wide, along.at[block])
            total = add_products(total)
        return total

    a1_sems, b1_sems = (a1_send, a1_recv), (b1_send, b1_recv)
    a2_sems, b2_sems = (a2_send, a2_recv), (b2_send, b2_recv)
    padded[...] = jnp.zeros_like(padded)
    loads[0].wait()
    pair_f = widen(pair_v)
    normed = norm(pair_f)
    loads[1].wait()
    mask[...] = tile_mask(row, col)
    mask_t[...] = tile_mask(col, row)
    loads[2].wait()
    left = gated(normed, w_ab1, 0, mask)
    right = gated(normed, w_ab1, 1, mask)
    a1_own[...] = pack(dot(turn[...], left))
    b1[col] = pack(dot(turn[...], right))

    @pl.when(mine)
    def _():
        pl.semaphore_wait(barrier, 2 * (n - 1))

    @pl.when(jnp.logical_not(mine))
    def _():
        pl.semaphore_wait(barrier, 2 * n - 1)

    turn_pair = send(pair_hbm, pair_t, t_send.at[0], t_recv.at[0], col, row)
    stay_pair = pltpu.make_async_copy(pair_hbm, pair_t, t_send.at[0])

    @pl.when(jnp.logical_not(mine))
    def _():
        turn_pair.start()

    @pl.when(mine)
    def _():
        stay_pair.start()

    spread_turned(a1_own, a1, a1_sems)
    spread_along(b1.at[col], b1, b1_sems)

    @pl.when(jnp.logical_not(mine))
    def _():
        turn_pair.wait_recv()

    @pl.when(mine)
    def _():
        stay_pair.wait()

    pair_f = widen(pair_t)
    normed = norm(pair_f)
    left_wide[...] = dot(turn[...], gated(normed, w_ab1, 0, mask_t)).reshape(left_wide.shape)
    loads[3].wait()
    gate = sigmoid(dot(normed, w_gate1[...]))
    total = contract(b1, right_wide, b1_sems, a1, left_wide, a1_sems)
    loads[4].wait()
    middle = finish(pair_f, total, gate, w_proj1)

    mid_own[...] = pack(middle.astype(jnp.float32))
    turn_mid = send(mid_own, mid_t, t_send.at[1], t_recv.at[1], col, row)

    normed = norm(middle.astype(jnp.float32))
    loads[5].wait()
    b2_own[...] = pack(gated(normed, w_ab2, 1, mask_t).astype(jnp.float32))
    spread_turned(b2_own, b2, b2_sems)

    @pl.when(jnp.logical_not(mine))
    def _():
        turn_mid.start()

    a2[col] = pack(gated(normed, w_ab2, 0, mask_t).astype(jnp.float32))
    spread_along(a2.at[col], a2, a2_sems)

    for copy in sends[: 2 * (n - 1)]:
        copy.wait_send()

    @pl.when(jnp.logical_not(mine))
    def _():
        turn_pair.wait_send()
        turn_mid.wait_send()
        turn_mid.wait_recv()

    @pl.when(mine)
    def _():
        mid_t[...] = mid_own[...]

    widen_block(padded, mid_t)
    mid_f = padded[...].reshape(side * wide, channels)
    normed = norm(mid_f)
    right_wide[...] = gated(normed, w_ab2, 1, mask).astype(jnp.float32).reshape(right_wide.shape)
    loads[6].wait()
    gate = sigmoid(dot(normed, w_gate2[...]))
    for copy in sends[2 * (n - 1) :]:
        copy.wait_send()
    total = contract(a2, left_wide, a2_sems, b2, right_wide, b2_sems)
    loads[7].wait()
    updated = finish(mid_f, total, gate, w_proj2)
    out_ref[...] = updated.reshape(side, wide, channels)[:, :side, :]


def on_square(n, pair, res_mask, *weights):
    side, _, channels = pair.shape
    wide = -(-side // 16) * 16
    block = pltpu.VMEM((side * side, channels), jnp.bfloat16)
    blocks = pltpu.VMEM((n, side * side, channels), jnp.bfloat16)
    positions = pltpu.VMEM((side, wide, channels), jnp.float32)
    tile = pltpu.VMEM(pair.shape, pair.dtype)
    sems = pltpu.SemaphoreType.DMA((n,))
    in_hbm = pl.BlockSpec(memory_space=pltpu.HBM)
    return pl.pallas_call(
        functools.partial(kernel, n, side, wide),
        out_shape=pltpu.VMEM(pair.shape, pair.dtype),
        in_specs=[in_hbm] * (2 + len(weights)),
        out_specs=pl.BlockSpec(memory_space=pltpu.VMEM),
        scratch_shapes=[tile, pltpu.SMEM(res_mask.shape, res_mask.dtype)]
        + [pltpu.VMEM(w.shape, w.dtype) for w in weights]
        + [positions] * 3
        + [pltpu.VMEM((side * wide, channels), jnp.float32)] * 2
        + [pltpu.VMEM((side * wide, side * wide), jnp.bfloat16)]
        + [tile, blocks, block, blocks]
        + [block, block, blocks, blocks, block]
        + [pltpu.SemaphoreType.DMA((2 + len(weights),))]
        + [pltpu.SemaphoreType.DMA((2,))] * 2
        + [sems] * 8,
        compiler_params=pltpu.CompilerParams(
            collective_id=0, has_side_effects=True, vmem_limit_bytes=60 * 2**20
        ),
    )(pair, res_mask, *weights)


def solution(mesh):
    n = mesh.shape["rows"]
    square = n == mesh.shape["chan"] * mesh.shape["sub"]

    def per_device(pair, *rest):
        if square and pair.shape[0] == pair.shape[1] == 12:
            return on_square(n, pair, *rest)
        return on_device(pair, *rest)

    return jax.shard_map(
        per_device,
        mesh=mesh,
        in_specs=(
            P(("groups", "rows"), ("chan", "sub"), None),
            P("groups"),
            P(),
            P(),
            P(),
            P(),
            P(),
            P(),
        ),
        out_specs=P(("groups", "rows"), ("chan", "sub"), None),
        check_vma=False,
    )
```
